128 devices in a mesh: dp: 32 (over y, x, core), mp: 4 (over z).
Axes of the slice: x: 4, y: 4, z: 4, core: 2. Of those that a mesh axis runs over, the one named last changes fastest.
Arguments:
- hidden: bfloat16 [1024, 8192], P('dp', 'mp'), may hold values from -6 to 6
- base_query_projection: bfloat16 [1024, 8192], P('dp', 'mp'), may hold values from -240 to 240
- adapter_owner_map: int32 [1024, 1], P('dp'), may hold values from 0 to 31; in each aligned block of 32 rows (0 to 31, 32 to 63, ...) at most 2 rows name the same one
- adapter_fetch_table: int32 [32, 32], P('dp'), may hold values from 0 to 3
- adapter_down_panels: bfloat16 [128, 64, 8192], P('dp', None, 'mp'), may hold values from -0.0625 to 0.0625
- adapter_up_panels: bfloat16 [128, 64, 8192], P('dp', None, 'mp'), may hold values from -0.75 to 0.75
- key_value_page_cache: bfloat16 [4096, 2, 128, 1024], P('dp', None, None, 'mp'), may hold values from -6 to 6
- request_page_table: int32 [1024, 4], P('dp'), may hold values from 0 to 159, as said below
- page_transfer_table: int32 [32, 32], P('dp'), may hold values from 0 to 127
- page_entry_mask: int32 [1024, 4], P('dp'), may hold values 0 or 1
- lengths: int32 [1024], P('dp'), may hold values from 1 to 512
- fresh_key_value: bfloat16 [1024, 2, 1024], P('dp', None, 'mp'), may hold values from -6 to 6
Outputs:
- attended: bfloat16 [1024, 8192], P('dp', 'mp')
The draws below stay inside these ranges and needn't reach their ends.
Inputs may be any that keep to these rules, and one draw needn't show every extreme that they name: `adapter_owner_map`: within each aligned block of 32 rows no owner is named by more than 2 rows, a bound that some block reaches. `request_page_table`: on each device the entries below 128 are distinct; an entry 128 + p stands at most once on a device and names the page listed in that device's row of page_transfer_table for owner p.
All inputs are finite; a program needn't handle non-finite values. No bound on the sum of `page_entry_mask` on one device may be relied on, other than what follows from the above.
Results may differ from the reference program's by a relative error of at most 0.025.
Values may be sent and summed in bfloat16 or wider, within the bound.
A program may use at most 192 MiB of HBM per device.

```python
import math
import jax
import jax.numpy as jnp
import numpy as np
from jax import lax

MODEL_WIDTH = 8192
H = 64
KVH = 8
HD = 128
ADAPTER_RANK = 64
PAGE = 128
MAXP = 4
REQ_DEV = 32
ADP_DEV = 4
MOST = 2
QUERY_WIDTH = 8192
REQUESTS = 1024
ADAPTER_COUNT = 128
PAGES_DEV = 128
POOL = 4096
N_DP = 32


def draw_base_query_projection(key, part):
    key = jax.random.fold_in(key, 3)
    values = jax.random.truncated_normal(key, -8.0, 8.0, (REQUESTS, QUERY_WIDTH), jnp.float32)
    return values.astype(jnp.bfloat16)


def draw_request_page_table(key, part):
    key = jax.random.fold_in(key, 7)
    entries = REQ_DEV * MAXP
    moved_count = min(N_DP, entries // 2)

    def one_device(device_key):
        first_key, second_key, third_key = jax.random.split(device_key, 3)
        entry_table = jax.random.permutation(first_key, entries).astype(jnp.int32)
        positions = jax.random.permutation(second_key, entries)[:moved_count]
        remote_slots = jax.random.permutation(third_key, N_DP)[:moved_count].astype(jnp.int32) + PAGES_DEV
        entry_table = entry_table.at[positions].set(remote_slots)
        return entry_table.reshape(REQ_DEV, MAXP)
    tables = jax.vmap(one_device)(jax.random.split(key, N_DP))
    return tables.reshape(REQUESTS, MAXP)


def plant(values, key, low, high):
    shape = values.shape
    place = [jax.random.randint(jax.random.fold_in(key, axis), (), 0, shape[axis]) for axis in range(len(shape))]
    values = values.at[tuple(place)].set(low)
    longest = shape.index(max(shape))
    place[longest] = (place[longest] + 1) % shape[longest]
    return values.at[tuple(place)].set(high)


def levels(key, dims, cuts, smallest, largest):
    loudness = 1.0
    for position, parts in cuts:
        steps = jax.random.uniform(jax.random.fold_in(jax.random.fold_in(key, 6), position), (parts,), jnp.float32, smallest / len(cuts), largest / len(cuts))
        loudness = loudness * jnp.repeat(jnp.exp(steps), dims[position] // parts).reshape((-1,) + (1,) * (len(dims) - 1 - position))
    return loudness


def assign_block(stream_key, own, number, rows, number_of, top, reach, lean):
    sequence = jax.random.permutation(stream_key, number_of)
    crowded, common = load_shares(number_of, rows * top, reach, lean, True), load_shares(number_of, rows * top, reach, lean, False)
    places = jnp.arange(number_of)

    def named(sizes, offset_by):
        used = int((sizes > 0).sum())
        fixed = max(1, used // 4)
        passed = fixed + (places - fixed + offset_by * (used - fixed)) % max(1, number_of - fixed)
        return jnp.zeros((number_of,), jnp.int32).at[sequence[jnp.where(places < fixed, places, passed)]].set(jnp.asarray(sizes, jnp.int32))

    sizes = jnp.where(number % 4 == 0, named(crowded, number // 4), named(common, number - number // 4 - 1))
    mixed = jax.random.permutation(jax.random.fold_in(own, 3), number_of)
    source_of, taker = mixed[0:number_of // 2 * 2:2], mixed[1:number_of // 2 * 2:2]
    slack = jnp.minimum(sizes[source_of] - 1, reach - sizes[taker]) // 2
    slack = jnp.where((source_of == sequence[0]) | (taker == sequence[0]) | (sizes[taker] == 0), 0, jnp.maximum(slack, 0))
    passed = jax.random.randint(jax.random.fold_in(own, 4), (number_of // 2,), 0, 1 << 20) % (slack + 1)
    sizes = sizes.at[source_of].add(-passed).at[taker].add(passed)
    members = jnp.searchsorted(jnp.cumsum(sizes), jnp.arange(rows * top), side="right").astype(jnp.int32)
    grid = members.reshape(top, rows).T
    grid = grid[jax.random.permutation(jax.random.fold_in(own, 1), rows)]
    offset_by = jax.random.randint(jax.random.fold_in(own, 2), (rows, 1), 0, top)
    return jnp.take_along_axis(grid, (jnp.arange(top)[None, :] + offset_by) % top, axis=1)


def load_shares(number_of, total, limit, lean, full):
    weights = [(1 << 20) // math.isqrt(grade ** lean) + 1 for grade in range(1, number_of + 1)]
    largest = limit if full else min(limit, max(-(-total // number_of), total * weights[0] // sum(weights)))
    least = 1 if total - largest >= number_of - 1 else 0
    given, rest = [largest] + [least] * (number_of - 1), total - largest - least * (number_of - 1)
    while rest > 0:
        free = [i for i in range(1, number_of) if given[i] < largest] or [i for i in range(1, number_of) if given[i] < limit]
        mass, remaining = sum([weights[i] for i in free]), rest
        for i in free:
            addition = min(limit - given[i], max(1, remaining * weights[i] // mass), rest)
            given[i] = given[i] + addition
            rest = rest - addition
    return np.array(given)


def centred(stream_key, extent, width, bound, pieces=(), kind=jnp.bfloat16):
    factor_of = levels(stream_key, extent, pieces, -0.22, 0.18) if pieces else 1.0
    values = jax.random.normal(stream_key, extent, jnp.float32) * width * factor_of
    return jnp.minimum(jnp.maximum(values, -bound), bound).astype(kind)


def setup_inputs(seed: int = 0) -> dict:
    seeds = jax.random.split(jax.random.key(seed), 13)
    hidden = centred(seeds[0], (REQUESTS, MODEL_WIDTH), 1.0, 6.0, ((0, 32), (1, 4)))
    base_query_projection = draw_base_query_projection(jax.random.fold_in(seeds[12], 71), 0)
    adapter_owner_map_keys = jax.random.split(jax.random.fold_in(seeds[2], 1), REQUESTS // REQ_DEV)
    adapter_owner_map_turns = jax.random.permutation(jax.random.fold_in(seeds[2], 3), REQUESTS // REQ_DEV)
    adapter_owner_map = jax.vmap(lambda own, number: assign_block(jax.random.fold_in(seeds[2], 2), own, number, REQ_DEV, N_DP, 1, MOST, 2))(adapter_owner_map_keys, adapter_owner_map_turns).reshape((REQUESTS, 1))
    adapter_fetch_table = plant(jax.random.randint(seeds[3], (N_DP, N_DP), 0, ADP_DEV), jax.random.fold_in(seeds[3], 1), 0, ADP_DEV - 1).astype(jnp.int32)
    adapter_down_panels = centred(seeds[4], (ADAPTER_COUNT, ADAPTER_RANK, MODEL_WIDTH), MODEL_WIDTH ** -0.5, 0.0625, ((0, 32), (2, 4)))
    adapter_up_panels = centred(seeds[5], (ADAPTER_COUNT, ADAPTER_RANK, QUERY_WIDTH), ADAPTER_RANK ** -0.5, 0.75, ((0, 32), (2, 4)))
    key_value_page_cache = centred(seeds[6], (POOL, 2, PAGE, KVH * HD), 1.0, 6.0, ((0, 32), (3, 4)))
    request_page_table = draw_request_page_table(jax.random.fold_in(seeds[12], 71), 0)
    page_transfer_table = plant(jax.random.randint(seeds[8], (N_DP, N_DP), 0, PAGES_DEV), jax.random.fold_in(seeds[8], 1), 0, PAGES_DEV - 1).astype(jnp.int32)
    page_entry_mask = plant((jax.random.randint(seeds[9], (REQUESTS, MAXP), 0, 4) < 3).astype(jnp.int32), jax.random.fold_in(seeds[9], 1), 0, 1)
    lengths = plant(jax.random.randint(seeds[10], (REQUESTS,), 1, MAXP * PAGE + 1), jax.random.fold_in(seeds[10], 1), 1, MAXP * PAGE).astype(jnp.int32)
    fresh_key_value = centred(seeds[11], (REQUESTS, 2, KVH * HD), 1.0, 6.0, ((0, 32), (2, 4)))
    return {"hidden": hidden, "base_query_projection": base_query_projection, "adapter_owner_map": adapter_owner_map, "adapter_fetch_table": adapter_fetch_table, "adapter_down_panels": adapter_down_panels, "adapter_up_panels": adapter_up_panels, "key_value_page_cache": key_value_page_cache, "request_page_table": request_page_table, "page_transfer_table": page_transfer_table, "page_entry_mask": page_entry_mask, "lengths": lengths, "fresh_key_value": fresh_key_value}


adapter_scale = 2.0
masked_score = -1e+30

def reference(hidden, base_query_projection, adapter_owner_map, adapter_fetch_table, adapter_down_panels, adapter_up_panels, key_value_page_cache, request_page_table, page_transfer_table, page_entry_mask, lengths, fresh_key_value):
    device = (jnp.arange(REQUESTS) // REQ_DEV).astype(jnp.int32)
    owner = adapter_owner_map[:, 0]
    adapter = (owner * ADP_DEV + adapter_fetch_table[device, owner]).astype(jnp.int32)
    remote = request_page_table >= PAGES_DEV
    slot = jnp.clip(request_page_table - PAGES_DEV, 0, N_DP - 1)
    global_page = jnp.where(remote, slot * PAGES_DEV + page_transfer_table[device[:, None], slot], device[:, None] * PAGES_DEV + request_page_table).astype(jnp.int32)
    group_size = H // KVH
    positions = jnp.arange(MAXP * PAGE)

    def one(items):
        hidden_input_row, base_query_row, adapter_number, pages, mask_row, length, fresh = items
        down_projected = jnp.dot(hidden_input_row[None, :], adapter_down_panels[adapter_number].T, preferred_element_type=jnp.float32).astype(jnp.bfloat16)
        query_update = jnp.dot(down_projected, adapter_up_panels[adapter_number], preferred_element_type=jnp.float32).astype(jnp.bfloat16)[0]
        adapted_query = (base_query_row.astype(jnp.float32) + adapter_scale * query_update.astype(jnp.float32)).astype(jnp.bfloat16)
        cache = key_value_page_cache[pages]
        keys = jnp.concatenate([cache[:, 0].reshape(MAXP * PAGE, KVH, HD), fresh[0].reshape(1, KVH, HD)], 0)
        values = jnp.concatenate([cache[:, 1].reshape(MAXP * PAGE, KVH, HD), fresh[1].reshape(1, KVH, HD)], 0)
        live = (mask_row[positions // PAGE] == 1) & (positions < length)
        live = jnp.concatenate([live, jnp.ones((1,), bool)])
        heads = adapted_query.reshape(KVH, group_size, HD).astype(jnp.float32)
        scores = jnp.einsum('gqd,tgd->gqt', heads, keys.astype(jnp.float32), precision=lax.Precision.HIGHEST) / math.sqrt(HD)
        scores = jnp.where(live, scores, masked_score)
        highest = lax.optimization_barrier(jnp.max(scores, axis=-1, keepdims=True))
        weights = jnp.where(live, jnp.exp(scores - highest), 0.0)
        total = lax.optimization_barrier(jnp.sum(weights, axis=-1))
        rounded = lax.optimization_barrier(weights.astype(jnp.bfloat16)).astype(jnp.float32)
        summed = jnp.einsum('gqt,tgd->gqd', rounded, values.astype(jnp.float32), precision=lax.Precision.HIGHEST)
        return (summed / total[..., None]).reshape(QUERY_WIDTH).astype(jnp.bfloat16)
    return lax.map(one, (hidden, base_query_projection, adapter, global_page, page_entry_mask, lengths, fresh_key_value))
```

```python
import functools
import math

import jax
import jax.numpy as jnp
from jax import lax
from jax.experimental import pallas as pl
from jax.experimental.pallas import tpu as pltpu
from jax.sharding import PartitionSpec as P

MESH = pl.DeviceIdType.MESH
BF, F32, I32 = jnp.bfloat16, jnp.float32, jnp.int32

N = 32
Z = 4
HD = 128
HEADS = 16
PAGE = 128
MAXP = 4
RANK = 64
CH = 8
CW = 256
ROWS = N * HEADS
SCALE = 1.0 / math.sqrt(HD)
LOW = -1e30
NT = (((1,), (1,)), ((), ()))


def iota(shape, dim):
    return lax.broadcasted_iota(I32, shape, dim)


def hot(mask):
    return jnp.where(mask, 1.0, 0.0).astype(BF)


def dot(a, b):
    return jnp.dot(a, b, preferred_element_type=F32)


def pieces(x):
    hi = x.astype(BF).astype(F32)
    mid = (x - hi).astype(BF).astype(F32)
    return hi, mid, x - hi - mid


def block_select(left, right, rows):
    low_heads = (iota((rows, 1), 0) & 8) == 0
    return jnp.where(low_heads, left, right)


def kernel(
    own_ref, fetch_ref, tab_ref, move_ref, mask_ref, len_ref, fresh_ref, tab_s,
    hid_hbm, base_hbm, down_hbm, up_hbm, cache_hbm,
    out_ref,
    hid, base, down, up, cache,
    hsend, hrecv, dsend, drecv, tsend, trecv, tsm, zbuf, qsend, qrecv, psend, precv,
    pm, pinv, ph, gm, qsel, ex, cx, st1, st2, tmask,
    qbd, qbs, fkv, sl, wl, ss, ws, ol, loc, locp,
    lsem, ssem, rsem,
):
    d0 = lax.axis_index("dp")
    z0 = lax.axis_index("mp")

    barrier = pltpu.get_barrier_semaphore()

    def greet(k, _):
        pl.semaphore_signal(
            barrier, inc=1, device_id={"dp": lax.rem(d0 + k, N)}, device_id_type=MESH
        )
        return 0

    lax.fori_loop(1, N, greet, 0)
    for k in range(1, Z):
        pl.semaphore_signal(
            barrier, inc=1, device_id={"mp": lax.rem(z0 + k, Z)}, device_id_type=MESH
        )

    cp_hid = pltpu.make_async_copy(hid_hbm, hid, lsem.at[0])
    cp_base = pltpu.make_async_copy(base_hbm, base, lsem.at[1])
    cp_down = pltpu.make_async_copy(down_hbm, down, lsem.at[2])
    cp_up = pltpu.make_async_copy(up_hbm, up, lsem.at[3])
    cp_cache = pltpu.make_async_copy(cache_hbm, cache, lsem.at[4])
    for cp in (cp_hid, cp_down, cp_up, cp_base, cp_cache):
        cp.start()

    def scatter(src, dst, rows, which):
        def body(k, _):
            t = lax.rem(d0 + k, N)
            pltpu.make_async_remote_copy(
                src_ref=src.at[pl.ds(pl.multiple_of(t * rows, rows), rows)],
                dst_ref=dst.at[pl.ds(pl.multiple_of(d0 * rows, rows), rows)],
                send_sem=ssem.at[which],
                recv_sem=rsem.at[which],
                device_id={"dp": t},
                device_id_type=MESH,
            ).start()
            return 0

        lax.fori_loop(1, N, body, 0)

    def drain(ref, rows, sem):
        part = ref.at[pl.ds(0, (N - 1) * rows)]
        pltpu.make_async_copy(part, part, sem).wait()

    def keep(src, dst, rows):
        here = pl.ds(pl.multiple_of(d0 * rows, rows), rows)
        dst[here, :] = src[here, :]

    ri, ci = iota((N, N), 0), iota((N, N), 1)
    rif, cif = ri.astype(F32), ci.astype(F32)

    def column(row):
        return jnp.sum(jnp.where(ri == ci, row, 0.0), axis=1, keepdims=True)

    own_r = own_ref[...].astype(F32)
    own_c = column(own_r)
    same = own_c == own_r
    rank_c = jnp.sum(jnp.where(same & (ci < ri), 1.0, 0.0), axis=1, keepdims=True)
    key_c = own_c * HEADS + rank_c * CH
    length = len_ref[...].astype(F32)
    fetch_c = column(fetch_ref[...].astype(F32))
    move_c = column(move_ref[...].astype(F32))
    req_c = jnp.zeros((N, 1), F32)
    nlp_c = jnp.zeros((N, 1), F32)
    remote = jnp.zeros((N, N), F32)
    local_live = []
    for j in range(MAXP):
        tab_r = tab_ref[j : j + 1, :].astype(F32)
        live_r = jnp.where(
            mask_ref[j : j + 1, :] == 1, jnp.clip(length - PAGE * j, 0.0, PAGE), 0.0
        )
        hit = tab_r == rif + PAGE
        req_c += jnp.sum(jnp.where(hit, cif + 1.0, 0.0), axis=1, keepdims=True)
        nlp_c += jnp.sum(jnp.where(hit, live_r, 0.0), axis=1, keepdims=True)
        local_live.append(column(jnp.where(tab_r < PAGE, live_r, 0.0)))
        remote += jnp.where(column(tab_r) == cif + PAGE, 1.0, 0.0)

    lane = iota((N, 128), 1)
    tsend[...] = jnp.where(
        lane == 0, fetch_c, jnp.where(lane == 1, move_c, jnp.where(lane == 2, nlp_c, 0.0))
    ).astype(I32)

    jj, rr = iota((N, CW), 1), iota((N, CW), 0)
    target = jnp.sum(
        jnp.where(rr == (jj & (N - 1)), key_c, 0.0), axis=0, keepdims=True
    ) + (jj[:1] >> 5).astype(F32)
    place = hot(iota((ROWS, CW), 0).astype(F32) == target)
    cp_hid.wait()
    chunks = jnp.concatenate([hid[:, c * CW : (c + 1) * CW] for c in range(CH)], axis=0)
    hsend[...] = dot(place, chunks).astype(BF)

    pl.semaphore_wait(barrier, N - 1 + Z - 1)
    scatter(hsend, hrecv, HEADS, 0)
    scatter(tsend, trecv, 1, 1)
    keep(hsend, hrecv, HEADS)
    keep(tsend, trecv, 1)

    blk = 64

    def rows_of(b):
        return pl.ds(pl.multiple_of(b * blk, blk), blk)

    vals = jnp.where(lane == 0, req_c, 0.0)
    for j in range(MAXP):
        vals = jnp.where(lane == j + 1, local_live[j], vals)
    tmask[...] = jnp.concatenate([remote, jnp.zeros((N, 128 - N), F32)], axis=1)
    vals = vals.astype(BF)
    for c in range(CH):
        gm[c * N : (c + 1) * N, :] = hot(iota((N, ROWS), 1).astype(F32) == key_c + float(c))

    def build(b, _):
        i = iota((blk, 1), 0) + b * blk
        j = iota((blk, ROWS), 1)
        at = rows_of(b)
        pm[at, :] = hot(j == ((i & 31) << 4) + (((i >> 5) & 1) << 3) + (i >> 6))
        pinv[at, :] = hot(j == ((i & 7) << 6) + (((i >> 3) & 1) << 5) + (i >> 4))
        ph[at, :] = hot(j == ((i & 31) << 4) + (i >> 5))
        head = ((i & 1) << 8) + (((i >> 1) & 7) << 5)
        e = hot(iota((blk, N), 1) == (i >> 4))
        ex[at, :] = e
        x = dot(e, vals)
        cx[at, :] = x
        req = x[:, 0:1]
        qsel[at, :] = hot(
            j.astype(F32) == jnp.where(req > 0.0, req - 1.0 + head.astype(F32), -1.0)
        )
        qsel[pl.ds(pl.multiple_of(ROWS + b * blk, blk), blk), :] = hot(j == head + (i >> 4))
        k0 = dot(hot(iota((blk, 2 * N), 1) == (i >> 4) * 2), fresh_ref[...])
        v0 = dot(hot(iota((blk, 2 * N), 1) == (i >> 4) * 2 + 1), fresh_ref[...])
        fkv[at, :] = jnp.concatenate(
            [
                block_select(k0[:, :HD], k0[:, HD:], blk),
                block_select(v0[:, :HD], v0[:, HD:], blk),
            ],
            axis=1,
        )
        return 0

    lax.fori_loop(0, ROWS // blk, build, 0)

    cp_down.wait()
    drain(trecv, 1, rsem.at[1])
    cp_tsm = pltpu.make_async_copy(trecv, tsm, lsem.at[5])
    cp_tsm.start()
    adapter = trecv[:, 0:1].astype(F32)
    adapter = jnp.concatenate([adapter, adapter], axis=0)
    wanted = (iota((2 * N, CW), 1) >> 6).astype(F32) == adapter
    drain(hrecv, HEADS, rsem.at[0])
    arranged = dot(pm[...], hrecv[...]).astype(BF)
    acc = jnp.zeros((2 * N, CW), F32)
    for c in range(CH):
        acc += lax.dot_general(
            arranged[c * 2 * N : (c + 1) * 2 * N],
            down[:, c * CW : (c + 1) * CW],
            NT,
            preferred_element_type=F32,
        )
    acc = jnp.where(wanted, acc, 0.0)
    zbuf[pl.ds(z0, 1)] = (acc[:, :128] + acc[:, 128:])[None]
    for k in range(1, Z):
        pltpu.make_async_remote_copy(
            src_ref=zbuf.at[z0],
            dst_ref=zbuf.at[z0],
            send_sem=ssem.at[2],
            recv_sem=rsem.at[2],
            device_id={"mp": lax.rem(z0 + k, Z)},
            device_id_type=MESH,
        ).start()
    zpart = zbuf.at[pl.ds(0, Z - 1)]
    cp_up.wait()
    pltpu.make_async_copy(zpart, zpart, rsem.at[2]).wait()
    u = (zbuf[0] + zbuf[1]) + (zbuf[2] + zbuf[3])
    u = jnp.where(wanted, jnp.concatenate([u, u], axis=1), 0.0).astype(BF)
    for c in range(CH):
        st1[c * 2 * N : (c + 1) * 2 * N, :] = dot(u, up[:, c * CW : (c + 1) * CW]).astype(BF)
    dsend[...] = dot(pinv[...], st1[...]).astype(BF)
    scatter(dsend, drecv, HEADS, 3)
    keep(dsend, drecv, HEADS)

    cp_base.wait()
    drain(drecv, HEADS, rsem.at[3])
    base_re = jnp.concatenate([base[:, c * CW : (c + 1) * CW] for c in range(CH)], axis=0)
    query = (base_re.astype(F32) + 2.0 * dot(gm[...], drecv[...])).astype(BF)
    st2[: CW, :] = query[:, :HD]
    st2[CW :, :] = query[:, HD:]
    qsend[...] = dot(qsel[:ROWS, :], st2[...]).astype(BF)
    scatter(qsend, qrecv, HEADS, 4)
    keep(qsend, qrecv, HEADS)
    query = dot(qsel[ROWS:, :], st2[...])
    qbd[:, :HD] = block_select(query, 0.0, ROWS).astype(BF)
    qbd[:, HD:] = block_select(0.0, query, ROWS).astype(BF)
    loc[:, 0:1] = jnp.sum(query * fkv[:, :HD], axis=1, keepdims=True) * SCALE

    cp_cache.wait()

    def local_scores(r, _):
        at = pl.ds(pl.multiple_of(r * HEADS, HEADS), HEADS)
        q = qbd[at, :]
        for j in range(MAXP):
            page = jnp.minimum(tab_s[j, r], PAGE - 1)
            sl[at, j * PAGE : (j + 1) * PAGE] = lax.dot_general(
                q, cache[page, 0], NT, preferred_element_type=F32
            )
        return 0

    lax.fori_loop(0, N, local_scores, 0, unroll=2)

    drain(qrecv, HEADS, rsem.at[4])
    cp_tsm.wait()
    got = qrecv[...].astype(F32)
    qbs[:, :HD] = block_select(got, 0.0, ROWS).astype(BF)
    qbs[:, HD:] = block_select(0.0, got, ROWS).astype(BF)

    def served_scores(d, _):
        at = pl.ds(pl.multiple_of(d * HEADS, HEADS), HEADS)
        page = jnp.clip(tsm[d, 1], 0, PAGE - 1)
        ss[at, :] = lax.dot_general(qbs[at, :], cache[page, 0], NT, preferred_element_type=F32)
        return 0

    lax.fori_loop(0, N, served_scores, 0, unroll=4)
    counts = trecv[...].astype(F32).astype(BF)

    def served_weights(b, _):
        at = rows_of(b)
        n_live = dot(ex[at, :], counts)[:, 2:3]
        live = iota((blk, PAGE), 1).astype(F32) < n_live
        s = jnp.where(live, ss[at, :] * SCALE, LOW)
        m = jnp.max(s, axis=1, keepdims=True)
        w = jnp.where(live, jnp.exp(s - m), 0.0)
        total = jnp.sum(w, axis=1, keepdims=True)
        ws[at, :] = w.astype(BF)
        some = total > 0.0
        total = jnp.where(some, total, 1.0)
        hi, mid, lo = pieces(jnp.where(some, m + jnp.log(total), LOW))
        at_lane = iota((blk, 128), 1)
        stat = jnp.where(at_lane == d0, hi, 0.0)
        stat = jnp.where(at_lane == d0 + N, mid, stat)
        stat = jnp.where(at_lane == d0 + 2 * N, lo, stat)
        psend[at, HD:] = stat.astype(BF)
        ss[at, :] = jnp.broadcast_to(1.0 / total, (blk, 128))
        return 0

    lax.fori_loop(0, ROWS // blk, served_weights, 0)

    def served_values(d, _):
        at = pl.ds(pl.multiple_of(d * HEADS, HEADS), HEADS)
        page = jnp.clip(tsm[d, 1], 0, PAGE - 1)
        o = dot(ws[at, :], cache[page, 1])
        psend[at, :HD] = (block_select(o[:, :HD], o[:, HD:], HEADS) * ss[at, :]).astype(BF)
        return 0

    lax.fori_loop(0, N, served_values, 0, unroll=4)
    scatter(psend, precv, HEADS, 5)
    keep(psend, precv, HEADS)

    def local_weights(b, _):
        at = rows_of(b)
        x = cx[at, :]
        fresh = loc[at, 0:1]
        t = iota((blk, PAGE), 1).astype(F32)
        parts, lives = [], []
        m = fresh
        for j in range(MAXP):
            live = t < x[:, j + 1 : j + 2]
            s = jnp.where(live, sl[at, j * PAGE : (j + 1) * PAGE] * SCALE, LOW)
            m = jnp.maximum(m, jnp.max(s, axis=1, keepdims=True))
            parts.append(s)
            lives.append(live)
        wf = jnp.exp(fresh - m)
        total = wf
        for j in range(MAXP):
            w = jnp.where(lives[j], jnp.exp(parts[j] - m), 0.0)
            total += jnp.sum(w, axis=1, keepdims=True)
            wl[at, j * PAGE : (j + 1) * PAGE] = w.astype(BF)
        at_lane = iota((blk, 128), 1)
        stat = jnp.where(at_lane == 0, m, jnp.where(at_lane == 1, total, 0.0))
        loc[at, :] = jnp.where(at_lane == 2, wf, stat)
        return 0

    lax.fori_loop(0, ROWS // blk, local_weights, 0)

    def local_values(r, _):
        at = pl.ds(pl.multiple_of(r * HEADS, HEADS), HEADS)
        o = jnp.zeros((HEADS, CW), F32)
        for j in range(MAXP):
            page = jnp.minimum(tab_s[j, r], PAGE - 1)
            o += dot(wl[at, j * PAGE : (j + 1) * PAGE], cache[page, 1])
        ol[at, :] = block_select(o[:, :HD], o[:, HD:], HEADS)
        return 0

    lax.fori_loop(0, N, local_values, 0, unroll=2)

    def local_part(b, _):
        at = rows_of(b)
        st = loc[at, :]
        m, total, wf = st[:, 0:1], st[:, 1:2], st[:, 2:3].astype(BF).astype(F32)
        o = (ol[at, :] + wf * fkv[at, HD:]) / total
        hi, mid, lo = pieces(m + jnp.log(total))
        at_lane = iota((blk, 128), 1)
        stat = jnp.where(at_lane == 0, hi, jnp.where(at_lane == 1, mid, 0.0))
        stat = jnp.where(at_lane == 2, lo, stat)
        locp[at, :HD] = o.astype(BF)
        locp[at, HD:] = stat.astype(BF)
        return 0

    lax.fori_loop(0, ROWS // blk, local_part, 0)
    mine = dot(ph[...], locp[...])
    ol[...] = mine[:, :HD]
    loc[...] = mine[:, HD:]

    drain(precv, HEADS, rsem.at[5])
    stats = jnp.zeros((HEADS, 128), F32)
    for p in range(N):
        stats += precv[p * HEADS : (p + 1) * HEADS, HD:].astype(F32)
    stats = stats[:, :N] + stats[:, N : 2 * N] + stats[:, 2 * N : 3 * N]
    reads = tmask[:, :N] > 0.0
    spread = hot(iota((N, ROWS), 0) == (iota((N, ROWS), 1) >> 4))
    lane_head = iota((N, ROWS), 1) & 15
    others = precv[:, :HD]
    for h in range(HEADS):
        at = slice(h * N, (h + 1) * N)
        lse = jnp.where(reads, jnp.broadcast_to(stats[h : h + 1, :], (N, N)), LOW)
        mst = loc[at, :]
        mine = mst[:, 0:1] + mst[:, 1:2] + mst[:, 2:3]
        top = jnp.maximum(jnp.max(lse, axis=1, keepdims=True), mine)
        w = jnp.where(reads, jnp.exp(lse - top), 0.0)
        wm = jnp.exp(mine - top)
        inv = 1.0 / (jnp.sum(w, axis=1, keepdims=True) + wm)
        wide = dot((w * inv).astype(BF), spread)
        wide = jnp.where(lane_head == h, wide, 0.0).astype(BF)
        o = dot(wide, others) + (wm * inv) * ol[at, :]
        out_ref[:, h * HD : (h + 1) * HD] = o.astype(BF)

    drain(hsend, HEADS, ssem.at[0])
    drain(tsend, 1, ssem.at[1])
    pltpu.make_async_copy(zpart, zpart, ssem.at[2]).wait()
    drain(dsend, HEADS, ssem.at[3])
    drain(qsend, HEADS, ssem.at[4])
    drain(psend, HEADS, ssem.at[5])


def shards(
    hidden,
    base_query_projection,
    adapter_owner_map,
    adapter_fetch_table,
    adapter_down_panels,
    adapter_up_panels,
    key_value_page_cache,
    request_page_table,
    page_transfer_table,
    page_entry_mask,
    lengths,
    fresh_key_value,
):
    width = N * 64
    table = request_page_table.T
    vmem = pl.BlockSpec(memory_space=pltpu.VMEM)
    smem = pl.BlockSpec(memory_space=pltpu.SMEM)
    hbm = pl.BlockSpec(memory_space=pl.ANY)
    v = pltpu.VMEM
    return pl.pallas_call(
        kernel,
        out_shape=jax.ShapeDtypeStruct((N, width), BF),
        in_specs=[vmem] * 7 + [smem] + [hbm] * 5,
        out_specs=vmem,
        scratch_shapes=[
            v((N, width), BF),
            v((N, width), BF),
            v((CW, width), BF),
            v((CW, width), BF),
            v((PAGE, 2, PAGE, CW), BF),
            v((ROWS, CW), BF),
            v((ROWS, CW), BF),
            v((ROWS, CW), BF),
            v((ROWS, CW), BF),
            v((N, 128), I32),
            v((N, 128), I32),
            pltpu.SMEM((N, 128), I32),
            v((Z, 2 * N, 128), F32),
            v((ROWS, HD), BF),
            v((ROWS, HD), BF),
            v((ROWS, CW), BF),
            v((ROWS, CW), BF),
            v((ROWS, ROWS), BF),
            v((ROWS, ROWS), BF),
            v((ROWS, ROWS), BF),
            v((CW, ROWS), BF),
            v((2 * ROWS, ROWS), BF),
            v((ROWS, N), BF),
            v((ROWS, 128), F32),
            v((ROWS, CW), BF),
            v((ROWS, HD), BF),
            v((N, 128), F32),
            v((ROWS, CW), BF),
            v((ROWS, CW), BF),
            v((ROWS, CW), F32),
            v((ROWS, ROWS), F32),
            v((ROWS, ROWS), BF),
            v((ROWS, PAGE), F32),
            v((ROWS, PAGE), BF),
            v((ROWS, HD), F32),
            v((ROWS, 128), F32),
            v((ROWS, CW), BF),
            pltpu.SemaphoreType.DMA((6,)),
            pltpu.SemaphoreType.DMA((6,)),
            pltpu.SemaphoreType.DMA((6,)),
        ],
        compiler_params=pltpu.CompilerParams(
            collective_id=0, has_side_effects=True, vmem_limit_bytes=50 * 1024 * 1024
        ),
    )(
        adapter_owner_map.T,
        adapter_fetch_table,
        table,
        page_transfer_table,
        page_entry_mask.T,
        lengths.reshape(1, N),
        fresh_key_value.reshape(2 * N, CW),
        table,
        hidden,
        base_query_projection,
        adapter_down_panels.reshape(CW, width),
        adapter_up_panels.reshape(CW, width),
        key_value_page_cache,
    )


def solution(mesh):
    return jax.shard_map(
        shards,
        mesh=mesh,
        in_specs=(
            P("dp", "mp"),
            P("dp", "mp"),
            P("dp", None),
            P("dp", None),
            P("dp", None, "mp"),
            P("dp", None, "mp"),
            P("dp", None, None, "mp"),
            P("dp", None),
            P("dp", None),
            P("dp", None),
            P("dp"),
            P("dp", None, "mp"),
        ),
        out_specs=P("dp", "mp"),
        check_vma=False,
    )
```

```python
import functools
import math

import jax
import jax.numpy as jnp
from jax import lax
from jax.experimental import pallas as pl
from jax.experimental.pallas import tpu as pltpu
from jax.sharding import PartitionSpec as P

MESH = pl.DeviceIdType.MESH
BF, F32, I32 = jnp.bfloat16, jnp.float32, jnp.int32

N = 32
Z = 4
HD = 128
HEADS = 16
PAGE = 128
MAXP = 4
RANK = 64
CH = 8
CW = 256
ROWS = N * HEADS
SCALE = 1.0 / math.sqrt(HD)
LOW = -1e30
NT = (((1,), (1,)), ((), ()))


def iota(shape, dim):
    return lax.broadcasted_iota(I32, shape, dim)


def hot(mask):
    return jnp.where(mask, 1.0, 0.0).astype(BF)


def dot(a, b):
    return jnp.dot(a, b, preferred_element_type=F32)


def pieces(x):
    hi = x.astype(BF).astype(F32)
    mid = (x - hi).astype(BF).astype(F32)
    return hi, mid, x - hi - mid


def block_select(left, right, rows):
    low_heads = (iota((rows, 1), 0) & 8) == 0
    return jnp.where(low_heads, left, right)


def kernel(
    own_hbm, fetch_hbm, tab_hbm, move_hbm, mask_hbm, len_hbm, fresh_hbm,
    hid_hbm, base_hbm, down_hbm, up_hbm, cache_hbm,
    out_ref,
    own_ref, fetch_ref, tab_ref, move_ref, mask_ref, len_ref, fresh_ref, tab_s,
    hid, base, down, up, cache,
    hsend, hrecv, dsend, drecv, tsend, trecv, tsm, zbuf,
    qsend, qrecv, psend, precv, lsend, lrecv,
    pm, pinv, ph, gm, qsel, ex, cx, st1, st2,
    qbd, fkv, sl, wl, lbias, sbias, mbias, ol, loc, locp,
    lsem, ssem, rsem, gsem,
):
    d0 = lax.axis_index("dp")
    z0 = lax.axis_index("mp")
    y0 = lax.div(d0, 8)
    x0 = lax.rem(d0, 8)

    barrier = pltpu.get_barrier_semaphore()

    def peers(dy, visit):
        row = lax.rem(y0 + dy, 4) * 8

        def body(k, _):
            visit(row + lax.rem(x0 + 4 + k + (lax.div(k, 4) if dy == 0 else 0), 8))
            return 0

        lax.fori_loop(0, 7 if dy == 0 else 8, body, 0)

    def greet(t):
        pl.semaphore_signal(barrier, inc=1, device_id={"dp": t}, device_id_type=MESH)

    for dy in (2, 1, 3, 0):
        peers(dy, greet)
    for k in range(1, Z):
        pl.semaphore_signal(
            barrier, inc=1, device_id={"mp": lax.rem(z0 + k, Z)}, device_id_type=MESH
        )

    cp_hid = pltpu.make_async_copy(hid_hbm, hid, lsem.at[0])
    cp_base = pltpu.make_async_copy(base_hbm, base, lsem.at[1])
    cp_down = pltpu.make_async_copy(down_hbm, down, lsem.at[2])
    cp_up = pltpu.make_async_copy(up_hbm, up, lsem.at[3])
    cp_cache = pltpu.make_async_copy(cache_hbm, cache, lsem.at[4])
    small = [
        pltpu.make_async_copy(src, dst, lsem.at[6 + i])
        for i, (src, dst) in enumerate((
            (own_hbm, own_ref), (fetch_hbm, fetch_ref), (tab_hbm, tab_ref),
            (move_hbm, move_ref), (mask_hbm, mask_ref), (len_hbm, len_ref),
            (fresh_hbm, fresh_ref), (tab_hbm, tab_s),
        ))
    ]
    for cp in (*small, cp_hid, cp_down, cp_up, cp_base, cp_cache):
        cp.start()

    def sender(src, dst, rows, send_sem, recv_sem):
        def visit(t):
            pltpu.make_async_remote_copy(
                src_ref=src.at[pl.ds(pl.multiple_of(t * rows, rows), rows)],
                dst_ref=dst.at[pl.ds(pl.multiple_of(d0 * rows, rows), rows)],
                send_sem=send_sem,
                recv_sem=recv_sem,
                device_id={"dp": t},
                device_id_type=MESH,
            ).start()

        return visit

    def scatter(src, dst, rows, which):
        for dy in (2, 1, 3, 0):
            peers(dy, sender(src, dst, rows, ssem.at[which], rsem.at[which]))

    def drain(ref, rows, sem, count=N - 1):
        part = ref.at[pl.ds(0, count * rows)]
        pltpu.make_async_copy(part, part, sem).wait()

    def keep(src, dst, rows):
        here = pl.ds(pl.multiple_of(d0 * rows, rows), rows)
        dst[here, :] = src[here, :]

    ri, ci = iota((N, N), 0), iota((N, N), 1)
    rif, cif = ri.astype(F32), ci.astype(F32)

    def column(row):
        return jnp.sum(jnp.where(ri == ci, row, 0.0), axis=1, keepdims=True)

    for cp in small[:6]:
        cp.wait()
    own_r = own_ref[...].astype(F32)
    own_c = column(own_r)
    same = own_c == own_r
    rank_c = jnp.sum(jnp.where(same & (ci < ri), 1.0, 0.0), axis=1, keepdims=True)
    key_c = own_c * HEADS + rank_c * CH
    length = len_ref[...].astype(F32)
    fetch_c = column(fetch_ref[...].astype(F32))
    move_c = column(move_ref[...].astype(F32))
    req_c = jnp.zeros((N, 1), F32)
    nlp_c = jnp.zeros((N, 1), F32)
    remote = jnp.zeros((N, N), F32)
    local_live = []
    for j in range(MAXP):
        tab_r = tab_ref[j : j + 1, :].astype(F32)
        live_r = jnp.where(
            mask_ref[j : j + 1, :] == 1, jnp.clip(length - PAGE * j, 0.0, PAGE), 0.0
        )
        hit = tab_r == rif + PAGE
        req_c += jnp.sum(jnp.where(hit, cif + 1.0, 0.0), axis=1, keepdims=True)
        nlp_c += jnp.sum(jnp.where(hit, live_r, 0.0), axis=1, keepdims=True)
        local_live.append(column(jnp.where(tab_r < PAGE, live_r, 0.0)))
        remote += jnp.where(column(tab_r) == cif + PAGE, 1.0, 0.0)

    lane = iota((N, 128), 1)
    tsend[...] = jnp.where(
        lane == 0, fetch_c, jnp.where(lane == 1, move_c, jnp.where(lane == 2, nlp_c, 0.0))
    ).astype(I32)

    jj, rr = iota((N, CW), 1), iota((N, CW), 0)
    target = jnp.sum(
        jnp.where(rr == (jj & (N - 1)), key_c, 0.0), axis=0, keepdims=True
    ) + (jj[:1] >> 5).astype(F32)
    place = hot(iota((ROWS, CW), 0).astype(F32) == target)
    cp_hid.wait()
    chunks = jnp.concatenate([hid[:, c * CW : (c + 1) * CW] for c in range(CH)], axis=0)
    hsend[...] = dot(place, chunks).astype(BF)

    pl.semaphore_wait(barrier, N - 1 + Z - 1)
    scatter(tsend, trecv, 1, 1)
    scatter(hsend, hrecv, HEADS, 0)
    keep(tsend, trecv, 1)
    keep(hsend, hrecv, HEADS)

    blk = 128

    def rows_of(b):
        return pl.ds(pl.multiple_of(b * blk, blk), blk)

    vals = jnp.where(lane == 0, req_c, 0.0)
    for j in range(MAXP):
        vals = jnp.where(lane == j + 1, local_live[j], vals)
    vals = vals.astype(BF)
    wide = jnp.concatenate([remote] * 4, axis=1)
    for h in range(4):
        mine = (iota((N, 128), 1) >> 5) == h
        mbias[h * N : (h + 1) * N, :] = jnp.where(mine & (wide > 0.0), 0.0, LOW)
    for c in range(CH):
        gm[c * N : (c + 1) * N, :] = hot(iota((N, ROWS), 1).astype(F32) == key_c + float(c))

    def build(b, _):
        i = iota((blk, 1), 0) + b * blk
        j = iota((blk, ROWS), 1)
        at = rows_of(b)
        pm[at, :] = hot(j == ((i & 31) << 4) + (((i >> 5) & 1) << 3) + (i >> 6))
        pinv[at, :] = hot(j == ((i & 7) << 6) + (((i >> 3) & 1) << 5) + (i >> 4))
        e = hot(iota((blk, N), 1) == (i >> 4))
        ex[at, :] = e
        cx[at, :] = dot(e, vals)
        return 0

    lax.fori_loop(0, ROWS // blk, build, 0)

    cp_down.wait()
    drain(trecv, 1, rsem.at[1])
    cp_tsm = pltpu.make_async_copy(trecv, tsm, lsem.at[5])
    cp_tsm.start()
    adapter = trecv[:, 0:1].astype(F32)
    adapter = jnp.concatenate([adapter, adapter], axis=0)
    wanted = (iota((2 * N, CW), 1) >> 6).astype(F32) == adapter
    drain(hrecv, HEADS, rsem.at[0])
    arranged = dot(pm[...], hrecv[...]).astype(BF)
    acc = jnp.zeros((2 * N, CW), F32)
    for c in range(CH):
        acc += lax.dot_general(
            arranged[c * 2 * N : (c + 1) * 2 * N],
            down[:, c * CW : (c + 1) * CW],
            NT,
            preferred_element_type=F32,
        )
    acc = jnp.where(wanted, acc, 0.0)
    zbuf[pl.ds(z0, 1)] = (acc[:, :128] + acc[:, 128:])[None]
    for k in (2, 1, 3):
        pltpu.make_async_remote_copy(
            src_ref=zbuf.at[z0],
            dst_ref=zbuf.at[z0],
            send_sem=ssem.at[2],
            recv_sem=rsem.at[2],
            device_id={"mp": lax.rem(z0 + k, Z)},
            device_id_type=MESH,
        ).start()
    zpart = zbuf.at[pl.ds(0, Z - 1)]

    small[6].wait()
    fresh = fresh_ref[...].reshape(2 * N, CW)

    def build_more(b, _):
        i = iota((blk, 1), 0) + b * blk
        j = iota((blk, ROWS), 1)
        at = rows_of(b)
        head = ((i & 1) << 8) + (((i >> 1) & 7) << 5)
        req = cx[at, 0:1]
        qsel[at, :] = hot(
            j.astype(F32) == jnp.where(req > 0.0, req - 1.0 + head.astype(F32), -1.0)
        )
        qsel[pl.ds(pl.multiple_of(ROWS + b * blk, blk), blk), :] = hot(j == head + (i >> 4))
        return 0

    lax.fori_loop(0, ROWS // blk, build_more, 0)
    cp_up.wait()
    pltpu.make_async_copy(zpart, zpart, rsem.at[2]).wait()
    u = (zbuf[0] + zbuf[1]) + (zbuf[2] + zbuf[3])
    u = jnp.where(wanted, jnp.concatenate([u, u], axis=1), 0.0).astype(BF)
    for c in range(CH):
        st1[c * 2 * N : (c + 1) * 2 * N, :] = dot(u, up[:, c * CW : (c + 1) * CW]).astype(BF)
    for dy in (2, 1, 3, 0):
        at = pl.ds(pl.multiple_of(lax.rem(y0 + dy, 4) * 128, 128), 128)
        dsend[at, :] = dot(pinv[at, :], st1[...]).astype(BF)
        peers(dy, sender(dsend, drecv, HEADS, ssem.at[3], rsem.at[3]))
    keep(dsend, drecv, HEADS)

    counts = trecv[...].astype(F32).astype(BF)

    def build_masks(b, _):
        i = iota((blk, 1), 0) + b * blk
        j = iota((blk, ROWS), 1)
        t = iota((blk, PAGE), 1).astype(F32)
        at = rows_of(b)
        ph[at, :] = hot(j == ((i & 31) << 4) + (i >> 5))
        n_live = dot(ex[at, :], counts)[:, 2:3]
        sbias[at, :] = jnp.where(t < n_live, 0.0, LOW)
        x = cx[at, :]
        for k in range(MAXP):
            lbias[at, k * PAGE : (k + 1) * PAGE] = jnp.where(t < x[:, k + 1 : k + 2], 0.0, LOW)
        k0 = dot(hot(iota((blk, 2 * N), 1) == (i >> 4) * 2), fresh)
        v0 = dot(hot(iota((blk, 2 * N), 1) == (i >> 4) * 2 + 1), fresh)
        fkv[at, :] = jnp.concatenate(
            [
                block_select(k0[:, :HD], k0[:, HD:], blk),
                block_select(v0[:, :HD], v0[:, HD:], blk),
            ],
            axis=1,
        )
        return 0

    lax.fori_loop(0, ROWS // blk, build_masks, 0)
    cp_base.wait()
    base_re = jnp.concatenate([base[:, c * CW : (c + 1) * CW] for c in range(CH)], axis=0)
    base_re = base_re.astype(F32)
    halves = iota((128, CW), 1) >> 7
    heads_of = hot(halves == ((iota((128, CW), 0) >> 3) & 1))

    drain(drecv, HEADS, rsem.at[3])
    query = (base_re + 2.0 * dot(gm[...], drecv[...])).astype(BF)
    st2[:CW, :] = query[:, :HD]
    st2[CW:, :] = query[:, HD:]
    for dy in (2, 1, 3, 0):
        at = pl.ds(pl.multiple_of(lax.rem(y0 + dy, 4) * 128, 128), 128)
        qsend[at, :] = dot(qsel[at, :], st2[...]).astype(BF)
        peers(dy, sender(qsend, qrecv, HEADS, ssem.at[4], gsem.at[dy]))
    keep(qsend, qrecv, HEADS)

    def spread_heads(q):
        return jnp.concatenate([q, q], axis=1) * heads_of

    for b in range(ROWS // 128):
        at = slice(b * 128, (b + 1) * 128)
        mine = dot(qsel[ROWS + b * 128 : ROWS + (b + 1) * 128, :], st2[...])
        qbd[at, :] = spread_heads(mine.astype(BF))
        loc[at, 0:1] = jnp.sum(mine * fkv[at, :HD], axis=1, keepdims=True) * SCALE

    cp_cache.wait()
    small[7].wait()

    def local_scores(r, _):
        at = pl.ds(pl.multiple_of(r * HEADS, HEADS), HEADS)
        q = qbd[at, :]
        for j in range(MAXP):
            page = jnp.minimum(tab_s[j, r], PAGE - 1)
            sl[at, j * PAGE : (j + 1) * PAGE] = lax.dot_general(
                q, cache[page, 0], NT, preferred_element_type=F32
            )
        return 0

    lax.fori_loop(0, N, local_scores, 0, unroll=8)

    cp_tsm.wait()
    for dy in (0, 1, 3, 2):
        row = lax.rem(y0 + 4 - dy, 4)
        at = pl.ds(pl.multiple_of(row * 128, 128), 128)
        drain(qrecv, HEADS, gsem.at[dy], 7 if dy == 0 else 8)
        q = spread_heads(qrecv[at, :])
        pages = [jnp.clip(tsm[row * 8 + i, 1], 0, PAGE - 1) for i in range(8)]
        s = jnp.concatenate(
            [
                lax.dot_general(
                    q[i * HEADS : (i + 1) * HEADS],
                    cache[pages[i], 0],
                    NT,
                    preferred_element_type=F32,
                )
                for i in range(8)
            ],
            axis=0,
        )
        s = s * SCALE + sbias[at, :]
        m = jnp.max(s, axis=1, keepdims=True)
        w = jnp.exp(s - m)
        total = jnp.sum(w, axis=1, keepdims=True)
        w = w.astype(BF)
        o = jnp.concatenate(
            [dot(w[i * HEADS : (i + 1) * HEADS], cache[pages[i], 1]) for i in range(8)], axis=0
        )
        psend[at, :] = (block_select(o[:, :HD], o[:, HD:], 128) / total).astype(BF)
        lse = jnp.where(
            iota((128, 128), 1) == (iota((128, 128), 0) & 15), m + jnp.log(total), 0.0
        )
        lsend[pl.ds(pl.multiple_of(row * 8, 8), 8), :] = jnp.sum(
            lse.reshape(8, HEADS, 128), axis=1
        )
        back = (4 - dy) % 4
        peers(back, sender(lsend, lrecv, 1, ssem.at[6], rsem.at[6]))
        peers(back, sender(psend, precv, HEADS, ssem.at[5], rsem.at[5]))
    keep(lsend, lrecv, 1)
    keep(psend, precv, HEADS)

    def local_weights(b, _):
        at = rows_of(b)
        new = loc[at, 0:1]
        parts = [
            sl[at, j * PAGE : (j + 1) * PAGE] * SCALE + lbias[at, j * PAGE : (j + 1) * PAGE]
            for j in range(MAXP)
        ]
        m = jnp.maximum(jnp.maximum(parts[0], parts[1]), jnp.maximum(parts[2], parts[3]))
        m = jnp.maximum(jnp.max(m, axis=1, keepdims=True), new)
        wf = jnp.exp(new - m)
        total = jnp.zeros((blk, PAGE), F32)
        for j in range(MAXP):
            w = jnp.exp(parts[j] - m)
            total += w
            wl[at, j * PAGE : (j + 1) * PAGE] = w.astype(BF)
        total = jnp.sum(total, axis=1, keepdims=True) + wf
        at_lane = iota((blk, 128), 1)
        stat = jnp.where(at_lane == 0, m, jnp.where(at_lane == 1, total, 0.0))
        loc[at, :] = jnp.where(at_lane == 2, wf, stat)
        return 0

    lax.fori_loop(0, ROWS // blk, local_weights, 0)

    def local_values(r, _):
        at = pl.ds(pl.multiple_of(r * HEADS, HEADS), HEADS)
        o = jnp.zeros((HEADS, CW), F32)
        for j in range(MAXP):
            page = jnp.minimum(tab_s[j, r], PAGE - 1)
            o += dot(wl[at, j * PAGE : (j + 1) * PAGE], cache[page, 1])
        ol[at, :] = block_select(o[:, :HD], o[:, HD:], HEADS)
        return 0

    lax.fori_loop(0, N, local_values, 0, unroll=8)

    def local_part(b, _):
        at = rows_of(b)
        st = loc[at, :]
        m, total, wf = st[:, 0:1], st[:, 1:2], st[:, 2:3].astype(BF).astype(F32)
        o = (ol[at, :] + wf * fkv[at, HD:]) / total
        hi, mid, lo = pieces(m + jnp.log(total))
        at_lane = iota((blk, 128), 1)
        stat = jnp.where(at_lane == 0, hi, jnp.where(at_lane == 1, mid, 0.0))
        stat = jnp.where(at_lane == 2, lo, stat)
        locp[at, :HD] = o.astype(BF)
        locp[at, HD:] = stat.astype(BF)
        return 0

    lax.fori_loop(0, ROWS // blk, local_part, 0)
    mine = dot(ph[...], locp[...])
    ol[...] = mine[:, :HD]
    loc[...] = jnp.broadcast_to(
        mine[:, HD : HD + 1] + mine[:, HD + 1 : HD + 2] + mine[:, HD + 2 : HD + 3], (ROWS, 128)
    )

    drain(lrecv, 1, rsem.at[6])
    stats = jnp.transpose(lrecv[...])
    drain(precv, HEADS, rsem.at[5])
    others = dot(ph[...], precv[...]).astype(BF)
    others = jnp.concatenate([others, jnp.ones((ROWS, 128), BF)], axis=1)
    for g in range(4):
        at = slice(g * 128, (g + 1) * 128)
        row = jnp.concatenate([stats[4 * g + i : 4 * g + i + 1, :] for i in range(4)], axis=1)
        lse = row + mbias[...]
        mine = loc[at, :]
        top = jnp.maximum(jnp.max(lse, axis=1, keepdims=True), mine)
        both = dot(jnp.exp(lse - top).astype(BF), others[at])
        wm = jnp.exp(mine - top)
        o = (both[:, :HD] + wm * ol[at, :]) / (both[:, HD:] + wm)
        for i in range(4):
            h = 4 * g + i
            out_ref[:, h * HD : (h + 1) * HD] = o[i * N : (i + 1) * N].astype(BF)

    drain(hsend, HEADS, ssem.at[0])
    drain(tsend, 1, ssem.at[1])
    pltpu.make_async_copy(zpart, zpart, ssem.at[2]).wait()
    drain(dsend, HEADS, ssem.at[3])
    drain(qsend, HEADS, ssem.at[4])
    drain(psend, HEADS, ssem.at[5])
    drain(lsend, 1, ssem.at[6])


def shards(
    hidden,
    base_query_projection,
    adapter_owner_map,
    adapter_fetch_table,
    adapter_down_panels,
    adapter_up_panels,
    key_value_page_cache,
    request_page_table,
    page_transfer_table,
    page_entry_mask,
    lengths,
    fresh_key_value,
):
    width = N * 64
    table = request_page_table.T
    vmem = pl.BlockSpec(memory_space=pltpu.VMEM)
    hbm = pl.BlockSpec(memory_space=pltpu.HBM)
    v = pltpu.VMEM
    return pl.pallas_call(
        kernel,
        out_shape=jax.ShapeDtypeStruct((N, width), BF),
        in_specs=[hbm] * 12,
        out_specs=vmem,
        scratch_shapes=[
            v((1, N), I32),
            v((1, N), I32),
            v((MAXP, N), I32),
            v((1, N), I32),
            v((MAXP, N), I32),
            v((1, N), I32),
            v((N, 2, CW), BF),
            pltpu.SMEM((MAXP, N), I32),
            v((N, width), BF),
            v((N, width), BF),
            v((CW, width), BF),
            v((CW, width), BF),
            v((PAGE, 2, PAGE, CW), BF),
            v((ROWS, CW), BF),
            v((ROWS, CW), BF),
            v((ROWS, CW), BF),
            v((ROWS, CW), BF),
            v((N, 128), I32),
            v((N, 128), I32),
            pltpu.SMEM((N, 128), I32),
            v((Z, 2 * N, 128), F32),
            v((ROWS, HD), BF),
            v((ROWS, HD), BF),
            v((ROWS, HD), BF),
            v((ROWS, HD), BF),
            v((N, 128), F32),
            v((N, 128), F32),
            v((ROWS, ROWS), BF),
            v((ROWS, ROWS), BF),
            v((ROWS, ROWS), BF),
            v((CW, ROWS), BF),
            v((2 * ROWS, ROWS), BF),
            v((ROWS, N), BF),
            v((ROWS, 128), F32),
            v((ROWS, CW), BF),
            v((ROWS, HD), BF),
            v((ROWS, CW), BF),
            v((ROWS, CW), F32),
            v((ROWS, ROWS), F32),
            v((ROWS, ROWS), BF),
            v((ROWS, ROWS), F32),
            v((ROWS, PAGE), F32),
            v((128, 128), F32),
            v((ROWS, HD), F32),
            v((ROWS, 128), F32),
            v((ROWS, CW), BF),
            pltpu.SemaphoreType.DMA((14,)),
            pltpu.SemaphoreType.DMA((7,)),
            pltpu.SemaphoreType.DMA((7,)),
            pltpu.SemaphoreType.DMA((4,)),
        ],
        compiler_params=pltpu.CompilerParams(
            collective_id=0, has_side_effects=True, vmem_limit_bytes=63 * 1024 * 1024
        ),
    )(
        adapter_owner_map.T,
        adapter_fetch_table,
        table,
        page_transfer_table,
        page_entry_mask.T,
        lengths.reshape(1, N),
        fresh_key_value,
        hidden,
        base_query_projection,
        adapter_down_panels.reshape(CW, width),
        adapter_up_panels.reshape(CW, width),
        key_value_page_cache,
    )


def solution(mesh):
    return jax.shard_map(
        shards,
        mesh=mesh,
        in_specs=(
            P("dp", "mp"),
            P("dp", "mp"),
            P("dp", None),
            P("dp", None),
            P("dp", None, "mp"),
            P("dp", None, "mp"),
            P("dp", None, None, "mp"),
            P("dp", None),
            P("dp", None),
            P("dp", None),
            P("dp"),
            P("dp", None, "mp"),
        ),
        out_specs=P("dp", "mp"),
        check_vma=False,
    )
```

```python
import functools
import math

import jax
import jax.numpy as jnp
from jax import lax
from jax.experimental import pallas as pl
from jax.experimental.pallas import tpu as pltpu
from jax.sharding import PartitionSpec as P

MESH = pl.DeviceIdType.MESH
BF, F32, I32 = jnp.bfloat16, jnp.float32, jnp.int32

N = 32
Z = 4
HD = 128
HEADS = 16
PAGE = 128
MAXP = 4
RANK = 64
CH = 8
CW = 256
ROWS = N * HEADS
FAR = (0, 1, 2, 1)
SCALE = 1.0 / math.sqrt(HD)
LOW = -1e30
NT = (((1,), (1,)), ((), ()))


def iota(shape, dim):
    return lax.broadcasted_iota(I32, shape, dim)


def hot(mask):
    return jnp.where(mask, 1.0, 0.0).astype(BF)


def dot(a, b):
    return jnp.dot(a, b, preferred_element_type=F32)


def pieces(x):
    hi = x.astype(BF).astype(F32)
    mid = (x - hi).astype(BF).astype(F32)
    return hi, mid, x - hi - mid


def block_select(left, right, rows):
    low_heads = (iota((rows, 1), 0) & 8) == 0
    return jnp.where(low_heads, left, right)


def kernel(
    own_hbm, fetch_hbm, tab_hbm, move_hbm, mask_hbm, len_hbm, fresh_hbm,
    hid_hbm, base_hbm, down_hbm, up_hbm, cache_hbm,
    out_ref,
    own_ref, fetch_ref, tab_ref, move_ref, mask_ref, len_ref, fresh_ref, tab_s,
    hid, base, down, up, cache, kt, kts,
    hsend, hrecv, dsend, drecv, tsend, trecv, tsm, zbuf,
    qsend, qrecv, psend, precv, lsend, lrecv,
    turn, ph, qsel, ex, cx, st1, basep, basel,
    qbd, fkv, sl, wl, lbias, sbias, mbias, ol, loc, locp,
    lsem, ssem, rsem, gsem,
):
    d0 = lax.axis_index("dp")
    z0 = lax.axis_index("mp")
    y0, x0, c0 = lax.div(d0, 8), lax.rem(lax.div(d0, 2), 4), lax.rem(d0, 2)
    rows8 = [lax.rem(y0 + dy, 4) * 8 for dy in range(4)]
    around = [[lax.rem(x0 + dx, 4) * 2 + c for c in (c0, 1 - c0)] for dx in range(4)]

    barrier = pltpu.get_barrier_semaphore()

    def peers(dy, visit):
        for dx in (2, 1, 3, 0):
            for dc in (1, 0):
                if (dy, dx, dc) != (0, 0, 0):
                    visit(rows8[dy] + around[dx][dc], FAR[dy] + FAR[dx])

    def greet(t, _):
        pl.semaphore_signal(barrier, inc=1, device_id={"dp": t}, device_id_type=MESH)

    for dy in (2, 1, 3, 0):
        peers(dy, greet)
    for k in range(1, Z):
        pl.semaphore_signal(
            barrier, inc=1, device_id={"mp": lax.rem(z0 + k, Z)}, device_id_type=MESH
        )

    cp_hid = pltpu.make_async_copy(hid_hbm, hid, lsem.at[0])
    cp_base = pltpu.make_async_copy(base_hbm, base, lsem.at[1])
    cp_down = pltpu.make_async_copy(down_hbm, down, lsem.at[2])
    cp_up = pltpu.make_async_copy(up_hbm, up, lsem.at[3])
    cp_cache = pltpu.make_async_copy(cache_hbm, cache, lsem.at[4])
    small = [
        pltpu.make_async_copy(src, dst, lsem.at[6 + i])
        for i, (src, dst) in enumerate((
            (own_hbm, own_ref), (fetch_hbm, fetch_ref), (tab_hbm, tab_ref),
            (move_hbm, move_ref), (mask_hbm, mask_ref), (len_hbm, len_ref),
            (fresh_hbm, fresh_ref), (tab_hbm, tab_s),
        ))
    ]
    for cp in (*small, cp_hid, cp_down, cp_up, cp_base, cp_cache):
        cp.start()

    def sender(src, dst, rows, send_sem, recv_sem, per_hops=None):
        def visit(t, hops):
            pltpu.make_async_remote_copy(
                src_ref=src.at[pl.ds(pl.multiple_of(t * rows, rows), rows)],
                dst_ref=dst.at[pl.ds(pl.multiple_of(d0 * rows, rows), rows)],
                send_sem=send_sem,
                recv_sem=recv_sem if per_hops is None else per_hops.at[hops],
                device_id={"dp": t},
                device_id_type=MESH,
            ).start()

        return visit

    def scatter(src, dst, rows, which):
        for dy in (2, 1, 3, 0):
            peers(dy, sender(src, dst, rows, ssem.at[which], rsem.at[which]))

    def drain(ref, rows, sem, count=N - 1):
        part = ref.at[pl.ds(0, count * rows)]
        pltpu.make_async_copy(part, part, sem).wait()

    def keep(src, dst, rows):
        here = pl.ds(pl.multiple_of(d0 * rows, rows), rows)
        dst[here, :] = src[here, :]

    ri, ci = iota((N, N), 0), iota((N, N), 1)
    rif, cif = ri.astype(F32), ci.astype(F32)

    def column(row):
        return jnp.sum(jnp.where(ri == ci, row, 0.0), axis=1, keepdims=True)

    for cp in small[:6]:
        cp.wait()
    own_r = own_ref[...].astype(F32)
    own_c = column(own_r)
    same = own_c == own_r
    rank_c = jnp.sum(jnp.where(same & (ci < ri), 1.0, 0.0), axis=1, keepdims=True)
    key_c = own_c * HEADS + rank_c * CH
    length = len_ref[...].astype(F32)
    fetch_c = column(fetch_ref[...].astype(F32))
    move_c = column(move_ref[...].astype(F32))
    req_c = jnp.zeros((N, 1), F32)
    nlp_c = jnp.zeros((N, 1), F32)
    slot_req_c = jnp.zeros((N, 1), F32)
    key_r = jnp.sum(jnp.where(ri == ci, key_c, 0.0), axis=0, keepdims=True)
    remote = jnp.zeros((N, N), F32)
    local_live = []
    for j in range(MAXP):
        tab_r = tab_ref[j : j + 1, :].astype(F32)
        live_r = jnp.where(
            mask_ref[j : j + 1, :] == 1, jnp.clip(length - PAGE * j, 0.0, PAGE), 0.0
        )
        hit = tab_r == rif + PAGE
        req_c += jnp.sum(jnp.where(hit, cif + 1.0, 0.0), axis=1, keepdims=True)
        slot_req_c += jnp.sum(jnp.where(hit, key_r / CH, 0.0), axis=1, keepdims=True)
        nlp_c += jnp.sum(jnp.where(hit, live_r, 0.0), axis=1, keepdims=True)
        local_live.append(column(jnp.where(tab_r < PAGE, live_r, 0.0)))
        remote += jnp.where(column(tab_r) == cif + PAGE, 1.0, 0.0)

    lane = iota((N, 128), 1)
    tsend[...] = jnp.where(
        lane == 0, fetch_c, jnp.where(lane == 1, move_c, jnp.where(lane == 2, nlp_c, 0.0))
    ).astype(I32)

    jj, rr = iota((N, CW), 1), iota((N, CW), 0)
    target = jnp.sum(
        jnp.where(rr == (jj & (N - 1)), key_c, 0.0), axis=0, keepdims=True
    ) + (jj[:1] >> 5).astype(F32)
    place = hot(iota((ROWS, CW), 0).astype(F32) == target)
    cp_hid.wait()
    chunks = jnp.concatenate([hid[:, c * CW : (c + 1) * CW] for c in range(CH)], axis=0)
    hsend[...] = dot(place, chunks).astype(BF)

    blk = 128

    def rows_of(b):
        return pl.ds(pl.multiple_of(b * blk, blk), blk)

    vals = jnp.where(lane == 0, req_c, 0.0)
    for j in range(MAXP):
        vals = jnp.where(lane == j + 1, local_live[j], vals)
    vals = jnp.where(lane == 5, slot_req_c, jnp.where(lane == 6, key_c / CH, vals))
    vals = vals.astype(BF)
    wide = jnp.concatenate([remote] * 4, axis=1)
    for h in range(4):
        mine = (iota((N, 128), 1) >> 5) == h
        mbias[h * N : (h + 1) * N, :] = jnp.where(mine & (wide > 0.0), 0.0, LOW)
    i128, j128 = iota((128, 128), 0), iota((128, 128), 1)
    turn[...] = hot(j128 == ((i128 & 7) << 4) + (((i128 >> 3) & 1) << 3) + (i128 >> 4))

    def build(b, _):
        i = iota((blk, 1), 0) + b * blk
        j = iota((blk, ROWS), 1)
        at = rows_of(b)
        e = hot(iota((blk, N), 1) == (i >> 4))
        ex[at, :] = e
        x = dot(e, vals)
        cx[at, :] = x
        chunk = (i >> 1) & 7
        jf = j.astype(F32)
        wants = x[:, 5:6] * CH + chunk.astype(F32)
        qsel[at, :] = hot(jf == jnp.where(x[:, 0:1] > 0.0, wants, -1.0))
        mine = x[:, 6:7] * CH + chunk.astype(F32)
        qsel[pl.ds(pl.multiple_of(ROWS + b * blk, blk), blk), :] = hot(jf == mine)
        return 0

    lax.fori_loop(0, ROWS // blk, build, 0)

    pl.semaphore_wait(barrier, N - 1 + Z - 1)
    scatter(hsend, hrecv, HEADS, 0)
    scatter(tsend, trecv, 1, 1)
    keep(tsend, trecv, 1)
    keep(hsend, hrecv, HEADS)

    cp_cache.wait()
    small[7].wait()

    def turn_local(r, _):
        for j in range(MAXP):
            page = jnp.minimum(tab_s[j, r], PAGE - 1)
            kt[r, :, j * PAGE : (j + 1) * PAGE] = jnp.transpose(cache[page, 0])
        return 0

    lax.fori_loop(0, N, turn_local, 0, unroll=4)

    cp_down.wait()
    drain(hrecv, HEADS, rsem.at[0])
    arranged = [
        dot(turn[...], hrecv[g * 128 : (g + 1) * 128, :]).astype(BF) for g in range(4)
    ]
    acc = jnp.zeros((2 * N, CW), F32)
    for c in range(CH):
        acc += lax.dot_general(
            jnp.concatenate([x[c * 16 : (c + 1) * 16] for x in arranged], axis=0),
            down[:, c * CW : (c + 1) * CW],
            NT,
            preferred_element_type=F32,
        )
    drain(trecv, 1, rsem.at[1])
    cp_tsm = pltpu.make_async_copy(trecv, tsm, lsem.at[5])
    cp_tsm.start()
    adapter = trecv[:, 0:1].astype(F32)
    adapter = jnp.concatenate(
        [adapter[g * 8 : (g + 1) * 8] for g in (0, 0, 1, 1, 2, 2, 3, 3)], axis=0
    )
    wanted = (iota((2 * N, CW), 1) >> 6).astype(F32) == adapter
    acc = jnp.where(wanted, acc, 0.0)
    zbuf[pl.ds(z0, 1)] = (acc[:, :128] + acc[:, 128:])[None]
    for k in (2, 1, 3):
        pltpu.make_async_remote_copy(
            src_ref=zbuf.at[z0],
            dst_ref=zbuf.at[z0],
            send_sem=ssem.at[2],
            recv_sem=rsem.at[2],
            device_id={"mp": lax.rem(z0 + k, Z)},
            device_id_type=MESH,
        ).start()
    zpart = zbuf.at[pl.ds(0, Z - 1)]

    cp_tsm.wait()

    def turn_served(d, _):
        kts[d] = jnp.transpose(cache[jnp.clip(tsm[d, 1], 0, PAGE - 1), 0])
        return 0

    lax.fori_loop(0, N, turn_served, 0, unroll=8)
    cp_up.wait()
    pltpu.make_async_copy(zpart, zpart, rsem.at[2]).wait()
    u = (zbuf[0] + zbuf[1]) + (zbuf[2] + zbuf[3])
    u = jnp.where(wanted, jnp.concatenate([u, u], axis=1), 0.0).astype(BF)
    deltas = [dot(u, up[:, c * CW : (c + 1) * CW]).astype(BF) for c in range(CH)]
    for g in range(4):
        st1[g * 128 : (g + 1) * 128, :] = jnp.concatenate(
            [x[g * 16 : (g + 1) * 16] for x in deltas], axis=0
        )
    for dy in (2, 1, 3, 0):
        at = pl.ds(pl.multiple_of(rows8[dy] * 16, 128), 128)
        dsend[at, :] = dot(turn[...], st1[at, :]).astype(BF)
        peers(dy, sender(dsend, drecv, HEADS, ssem.at[3], rsem.at[3]))
    keep(dsend, drecv, HEADS)

    small[6].wait()
    fresh = fresh_ref[...].reshape(2 * N, CW)
    counts = trecv[...].astype(F32).astype(BF)

    def build_masks(b, _):
        i = iota((blk, 1), 0) + b * blk
        j = iota((blk, ROWS), 1)
        t = iota((blk, PAGE), 1).astype(F32)
        at = rows_of(b)
        ph[at, :] = hot(j == ((i & 31) << 4) + (i >> 5))
        n_live = dot(ex[at, :], counts)[:, 2:3]
        sbias[at, :] = jnp.where(t < n_live, 0.0, LOW)
        x = cx[at, :]
        for k in range(MAXP):
            lbias[at, k * PAGE : (k + 1) * PAGE] = jnp.where(t < x[:, k + 1 : k + 2], 0.0, LOW)
        k0 = dot(hot(iota((blk, 2 * N), 1) == (i >> 4) * 2), fresh)
        v0 = dot(hot(iota((blk, 2 * N), 1) == (i >> 4) * 2 + 1), fresh)
        fkv[at, :] = jnp.concatenate(
            [
                block_select(k0[:, :HD], k0[:, HD:], blk),
                block_select(v0[:, :HD], v0[:, HD:], blk),
            ],
            axis=1,
        )
        return 0

    lax.fori_loop(0, ROWS // blk, build_masks, 0)
    cp_base.wait()
    chunked = jnp.concatenate([base[:, c * CW : (c + 1) * CW] for c in range(CH)], axis=0)

    def build_base(b, _):
        i = iota((blk, 1), 0) + b * blk
        j = iota((blk, CW), 1)
        at = rows_of(b)
        head = ((i >> 1) & 7) << 5
        req = cx[at, 0:1]
        want = jnp.where(req > 0.0, req - 1.0 + head.astype(F32), -1.0)
        both = dot(hot(j.astype(F32) == want), chunked)
        basep[at, :] = jnp.where((i & 1) == 0, both[:, :HD], both[:, HD:])
        both = dot(hot(j == head + (i >> 4)), chunked)
        basel[at, :] = jnp.where((i & 1) == 0, both[:, :HD], both[:, HD:])
        return 0

    lax.fori_loop(0, ROWS // blk, build_base, 0)
    odd = (iota((128, 1), 0) & 1) == 1
    halves = iota((HEADS, CW), 1) >> 7
    heads_of = hot(halves == ((iota((HEADS, CW), 0) >> 3) & 1))

    drain(drecv, HEADS, rsem.at[3])

    def pick(selector, base_rows):
        both = dot(selector, drecv[...])
        return (base_rows + 2.0 * jnp.where(odd, both[:, HD:], both[:, :HD])).astype(BF)

    for dy in (2, 1, 3, 0):
        at = pl.ds(pl.multiple_of(rows8[dy] * 16, 128), 128)
        qsend[at, :] = pick(qsel[at, :], basep[at, :])
        peers(dy, sender(qsend, qrecv, HEADS, ssem.at[4], None, gsem))
    keep(qsend, qrecv, HEADS)

    def spread_heads(q):
        return jnp.concatenate([q, q], axis=1) * jnp.concatenate([heads_of] * (q.shape[0] // HEADS), axis=0)

    for b in range(ROWS // 128):
        at = slice(b * 128, (b + 1) * 128)
        mine = pick(qsel[ROWS + b * 128 : ROWS + (b + 1) * 128, :], basel[at, :])
        qbd[at, :] = spread_heads(mine)
        loc[at, 0:1] = jnp.sum(mine.astype(F32) * fkv[at, :HD], axis=1, keepdims=True) * SCALE

    def local_scores(r, _):
        at = pl.ds(pl.multiple_of(r * HEADS, HEADS), HEADS)
        sl[at, :] = dot(qbd[at, :], kt[r])
        return 0


    def local_weights(b):
        at = slice(b * 256, (b + 1) * 256)
        new = loc[at, 0:1]
        parts = [
            sl[at, j * PAGE : (j + 1) * PAGE] * SCALE + lbias[at, j * PAGE : (j + 1) * PAGE]
            for j in range(MAXP)
        ]
        m = jnp.maximum(jnp.maximum(parts[0], parts[1]), jnp.maximum(parts[2], parts[3]))
        m = jnp.maximum(jnp.max(m, axis=1, keepdims=True), new)
        wf = jnp.exp(new - m)
        total = jnp.zeros((256, PAGE), F32)
        for j in range(MAXP):
            w = jnp.exp(parts[j] - m)
            total += w
            wl[at, j * PAGE : (j + 1) * PAGE] = w.astype(BF)
        total = jnp.sum(total, axis=1, keepdims=True) + wf
        at_lane = iota((256, 128), 1)
        stat = jnp.where(at_lane == 0, m, jnp.where(at_lane == 1, total, 0.0))
        loc[at, :] = jnp.where(at_lane == 2, wf, stat)

    def serve(*hops):
        slots = [d0] if 0 in hops else []
        for dist in hops:
            near = [
                rows8[dy] + around[dx][dc]
                for dy in range(4)
                for dx in range(4)
                for dc in range(2)
                if FAR[dy] + FAR[dx] == dist and (dy, dx, dc) != (0, 0, 0)
            ]
            drain(qrecv, HEADS, gsem.at[dist], len(near))
            slots += near
        n = len(slots) * HEADS
        ats = [pl.ds(pl.multiple_of(slot * HEADS, HEADS), HEADS) for slot in slots]
        s = [dot(spread_heads(qrecv[at, :]), kts[slot]) for at, slot in zip(ats, slots)]
        bias = jnp.concatenate([sbias[at, :] for at in ats], axis=0)
        s = jnp.concatenate(s, axis=0) * SCALE + bias
        m = jnp.max(s, axis=1, keepdims=True)
        w = jnp.exp(s - m)
        total = jnp.sum(w, axis=1, keepdims=True)
        w = w.astype(BF)
        o = [
            dot(
                w[i * HEADS : (i + 1) * HEADS],
                cache[jnp.clip(tsm[slot, 1], 0, PAGE - 1), 1],
            )
            for i, slot in enumerate(slots)
        ]
        o = jnp.concatenate(o, axis=0)
        o = (block_select(o[:, :HD], o[:, HD:], n) / total).astype(BF)
        lse = jnp.where(
            iota((n, 128), 1) == (iota((n, 128), 0) & 15), m + jnp.log(total), 0.0
        )
        lse = jnp.sum(lse.reshape(n // HEADS, HEADS, 128), axis=1)
        for i, slot in enumerate(slots):
            lsend[pl.ds(slot, 1), :] = lse[i : i + 1]
            psend[ats[i], :] = o[i * HEADS : (i + 1) * HEADS]
        for slot in slots[1 if 0 in hops else 0 :]:
            sender(lsend, lrecv, 1, ssem.at[6], rsem.at[6])(slot, None)
            sender(psend, precv, HEADS, ssem.at[5], rsem.at[5])(slot, None)

    lax.fori_loop(0, N // 2, local_scores, 0, unroll=8)
    serve(0, 1, 2)
    serve(3)
    serve(4)
    keep(lsend, lrecv, 1)
    keep(psend, precv, HEADS)

    lax.fori_loop(N // 2, N, local_scores, 0, unroll=8)
    local_weights(0)
    local_weights(1)

    def local_values(r, _):
        at = pl.ds(pl.multiple_of(r * HEADS, HEADS), HEADS)
        o = jnp.zeros((HEADS, CW), F32)
        for j in range(MAXP):
            page = jnp.minimum(tab_s[j, r], PAGE - 1)
            o += dot(wl[at, j * PAGE : (j + 1) * PAGE], cache[page, 1])
        ol[at, :] = block_select(o[:, :HD], o[:, HD:], HEADS)
        return 0

    lax.fori_loop(0, N, local_values, 0, unroll=8)

    def local_part(b, _):
        at = rows_of(b)
        st = loc[at, :]
        m, total, wf = st[:, 0:1], st[:, 1:2], st[:, 2:3].astype(BF).astype(F32)
        o = (ol[at, :] + wf * fkv[at, HD:]) / total
        hi, mid, lo = pieces(m + jnp.log(total))
        at_lane = iota((blk, 128), 1)
        stat = jnp.where(at_lane == 0, hi, jnp.where(at_lane == 1, mid, 0.0))
        stat = jnp.where(at_lane == 2, lo, stat)
        locp[at, :HD] = o.astype(BF)
        locp[at, HD:] = stat.astype(BF)
        return 0

    lax.fori_loop(0, ROWS // blk, local_part, 0, unroll=4)
    mine = dot(ph[...], locp[...])
    ol[...] = mine[:, :HD]
    loc[...] = jnp.broadcast_to(
        mine[:, HD : HD + 1] + mine[:, HD + 1 : HD + 2] + mine[:, HD + 2 : HD + 3], (ROWS, 128)
    )

    drain(lrecv, 1, rsem.at[6])
    stats = jnp.transpose(lrecv[...])
    drain(precv, HEADS, rsem.at[5])
    others = dot(ph[...], precv[...]).astype(BF)
    others = jnp.concatenate([others, jnp.ones((ROWS, 128), BF)], axis=1)
    for g in range(4):
        at = slice(g * 128, (g + 1) * 128)
        row = jnp.concatenate([stats[4 * g + i : 4 * g + i + 1, :] for i in range(4)], axis=1)
        lse = row + mbias[...]
        mine = loc[at, :]
        top = jnp.maximum(jnp.max(lse, axis=1, keepdims=True), mine)
        both = dot(jnp.exp(lse - top).astype(BF), others[at])
        wm = jnp.exp(mine - top)
        o = (both[:, :HD] + wm * ol[at, :]) / (both[:, HD:] + wm)
        for i in range(4):
            h = 4 * g + i
            out_ref[:, h * HD : (h + 1) * HD] = o[i * N : (i + 1) * N].astype(BF)

    drain(hsend, HEADS, ssem.at[0])
    drain(tsend, 1, ssem.at[1])
    pltpu.make_async_copy(zpart, zpart, ssem.at[2]).wait()
    drain(dsend, HEADS, ssem.at[3])
    drain(qsend, HEADS, ssem.at[4])
    drain(psend, HEADS, ssem.at[5])
    drain(lsend, 1, ssem.at[6])


def shards(
    hidden,
    base_query_projection,
    adapter_owner_map,
    adapter_fetch_table,
    adapter_down_panels,
    adapter_up_panels,
    key_value_page_cache,
    request_page_table,
    page_transfer_table,
    page_entry_mask,
    lengths,
    fresh_key_value,
):
    width = N * 64
    table = request_page_table.T
    vmem = pl.BlockSpec(memory_space=pltpu.VMEM)
    hbm = pl.BlockSpec(memory_space=pltpu.HBM)
    v = pltpu.VMEM
    return pl.pallas_call(
        kernel,
        out_shape=jax.ShapeDtypeStruct((N, width), BF),
        in_specs=[hbm] * 12,
        out_specs=vmem,
        scratch_shapes=[
            v((1, N), I32),
            v((1, N), I32),
            v((MAXP, N), I32),
            v((1, N), I32),
            v((MAXP, N), I32),
            v((1, N), I32),
            v((N, 2, CW), BF),
            pltpu.SMEM((MAXP, N), I32),
            v((N, width), BF),
            v((N, width), BF),
            v((CW, width), BF),
            v((CW, width), BF),
            v((PAGE, 2, PAGE, CW), BF),
            v((N, CW, MAXP * PAGE), BF),
            v((N, CW, PAGE), BF),
            v((ROWS, CW), BF),
            v((ROWS, CW), BF),
            v((ROWS, CW), BF),
            v((ROWS, CW), BF),
            v((N, 128), I32),
            v((N, 128), I32),
            pltpu.SMEM((N, 128), I32),
            v((Z, 2 * N, 128), F32),
            v((ROWS, HD), BF),
            v((ROWS, HD), BF),
            v((ROWS, HD), BF),
            v((ROWS, HD), BF),
            v((N, 128), F32),
            v((N, 128), F32),
            v((128, 128), BF),
            v((ROWS, ROWS), BF),
            v((2 * ROWS, ROWS), BF),
            v((ROWS, N), BF),
            v((ROWS, 128), F32),
            v((ROWS, CW), BF),
            v((ROWS, HD), F32),
            v((ROWS, HD), F32),
            v((ROWS, CW), BF),
            v((ROWS, CW), F32),
            v((ROWS, ROWS), F32),
            v((ROWS, ROWS), BF),
            v((ROWS, ROWS), F32),
            v((ROWS, PAGE), F32),
            v((128, 128), F32),
            v((ROWS, HD), F32),
            v((ROWS, 128), F32),
            v((ROWS, CW), BF),
            pltpu.SemaphoreType.DMA((14,)),
            pltpu.SemaphoreType.DMA((7,)),
            pltpu.SemaphoreType.DMA((7,)),
            pltpu.SemaphoreType.DMA((5,)),
        ],
        compiler_params=pltpu.CompilerParams(
            collective_id=0, has_side_effects=True, vmem_limit_bytes=63 * 1024 * 1024
        ),
    )(
        adapter_owner_map.T,
        adapter_fetch_table,
        table,
        page_transfer_table,
        page_entry_mask.T,
        lengths.reshape(1, N),
        fresh_key_value,
        hidden,
        base_query_projection,
        adapter_down_panels.reshape(CW, width),
        adapter_up_panels.reshape(CW, width),
        key_value_page_cache,
    )


def solution(mesh):
    return jax.shard_map(
        shards,
        mesh=mesh,
        in_specs=(
            P("dp", "mp"),
            P("dp", "mp"),
            P("dp", None),
            P("dp", None),
            P("dp", None, "mp"),
            P("dp", None, "mp"),
            P("dp", None, None, "mp"),
            P("dp", None),
            P("dp", None),
            P("dp", None),
            P("dp"),
            P("dp", None, "mp"),
        ),
        out_specs=P("dp", "mp"),
        check_vma=False,
    )
```

```python
import functools
import math

import jax
import jax.numpy as jnp
from jax import lax
from jax.experimental import pallas as pl
from jax.experimental.pallas import tpu as pltpu
from jax.sharding import PartitionSpec as P

MESH = pl.DeviceIdType.MESH
BF, F32, I32 = jnp.bfloat16, jnp.float32, jnp.int32

N = 32
Z = 4
HD = 128
HEADS = 16
PAGE = 128
MAXP = 4
RANK = 64
CH = 8
CW = 256
ROWS = N * HEADS
FAR = (0, 1, 2, 1)
SCALE = 1.0 / math.sqrt(HD)
LOW = -1e30
NT = (((1,), (1,)), ((), ()))


def iota(shape, dim):
    return lax.broadcasted_iota(I32, shape, dim)


def hot(mask):
    return jnp.where(mask, 1.0, 0.0).astype(BF)


def dot(a, b):
    return jnp.dot(a, b, preferred_element_type=F32)


def pieces(x):
    hi = x.astype(BF).astype(F32)
    mid = (x - hi).astype(BF).astype(F32)
    return hi, mid, x - hi - mid


def swap(x):
    return jnp.concatenate([x[:, RANK:], x[:, :RANK]], axis=1)


def block_select(left, right, rows):
    low_heads = (iota((rows, 1), 0) & 8) == 0
    return jnp.where(low_heads, left, right)


def kernel(
    own_hbm, fetch_hbm, tab_hbm, move_hbm, mask_hbm, len_hbm, fresh_hbm,
    hid_hbm, base_hbm, down_hbm, up_hbm, cache_hbm,
    out_ref,
    own_ref, fetch_ref, tab_ref, move_ref, mask_ref, len_ref, fresh_ref, tab_s,
    hid, base, down, up, cache, kt, kts,
    hsend, hrecv, dsend, drecv, tsend, trecv, tsm, zbuf,
    qsend, qrecv, psend, precv, lsend, lrecv,
    turn, ph, qsel, ex, cx, st1, basep, basel,
    qbd, fkv, sl, wl, lbias, sbias, mbias, ol, loc, locp,
    lsem, ssem, rsem, gsem,
):
    d0 = lax.axis_index("dp")
    z0 = lax.axis_index("mp")
    y0, x0, c0 = lax.div(d0, 8), lax.rem(lax.div(d0, 2), 4), lax.rem(d0, 2)
    rows8 = [lax.rem(y0 + dy, 4) * 8 for dy in range(4)]
    around = [[lax.rem(x0 + dx, 4) * 2 + c for c in (c0, 1 - c0)] for dx in range(4)]

    barrier = pltpu.get_barrier_semaphore()

    def peers(dy, visit):
        for dx in (2, 1, 3, 0):
            for dc in (1, 0):
                if (dy, dx, dc) != (0, 0, 0):
                    visit(rows8[dy] + around[dx][dc], FAR[dy] + FAR[dx])

    def greet(t, _):
        pl.semaphore_signal(barrier, inc=1, device_id={"dp": t}, device_id_type=MESH)

    for dy in (2, 1, 3, 0):
        peers(dy, greet)
    for k in range(1, Z):
        pl.semaphore_signal(
            barrier, inc=1, device_id={"mp": lax.rem(z0 + k, Z)}, device_id_type=MESH
        )

    cp_hid = pltpu.make_async_copy(hid_hbm, hid, lsem.at[0])
    cp_base = pltpu.make_async_copy(base_hbm, base, lsem.at[1])
    cp_down = pltpu.make_async_copy(down_hbm, down, lsem.at[2])
    cp_up = pltpu.make_async_copy(up_hbm, up, lsem.at[3])
    cp_cache = pltpu.make_async_copy(cache_hbm, cache, lsem.at[4])
    small = [
        pltpu.make_async_copy(src, dst, lsem.at[6 + i])
        for i, (src, dst) in enumerate((
            (own_hbm, own_ref), (fetch_hbm, fetch_ref), (tab_hbm, tab_ref),
            (move_hbm, move_ref), (mask_hbm, mask_ref), (len_hbm, len_ref),
            (fresh_hbm, fresh_ref), (tab_hbm, tab_s),
        ))
    ]
    for cp in (*small, cp_hid, cp_down, cp_up, cp_base, cp_cache):
        cp.start()

    def sender(src, dst, rows, send_sem, recv_sem, per_hops=None):
        def visit(t, hops):
            pltpu.make_async_remote_copy(
                src_ref=src.at[pl.ds(pl.multiple_of(t * rows, rows), rows)],
                dst_ref=dst.at[pl.ds(pl.multiple_of(d0 * rows, rows), rows)],
                send_sem=send_sem,
                recv_sem=recv_sem if per_hops is None else per_hops.at[hops],
                device_id={"dp": t},
                device_id_type=MESH,
            ).start()

        return visit

    def scatter(src, dst, rows, which):
        for dy in (2, 1, 3, 0):
            peers(dy, sender(src, dst, rows, ssem.at[which], rsem.at[which]))

    def drain(ref, rows, sem, count=N - 1):
        part = ref.at[pl.ds(0, count * rows)]
        pltpu.make_async_copy(part, part, sem).wait()

    def keep(src, dst, rows):
        here = pl.ds(pl.multiple_of(d0 * rows, rows), rows)
        dst[here, :] = src[here, :]

    ri, ci = iota((N, N), 0), iota((N, N), 1)
    rif, cif = ri.astype(F32), ci.astype(F32)

    def column(row):
        return jnp.sum(jnp.where(ri == ci, row, 0.0), axis=1, keepdims=True)

    for cp in small[:6]:
        cp.wait()
    own_r = own_ref[...].astype(F32)
    own_c = column(own_r)
    same = own_c == own_r
    rank_c = jnp.sum(jnp.where(same & (ci < ri), 1.0, 0.0), axis=1, keepdims=True)
    key_c = own_c * HEADS + rank_c * CH
    length = len_ref[...].astype(F32)
    fetch_c = column(fetch_ref[...].astype(F32))
    move_c = column(move_ref[...].astype(F32))
    req_c = jnp.zeros((N, 1), F32)
    nlp_c = jnp.zeros((N, 1), F32)
    slot_req_c = jnp.zeros((N, 1), F32)
    key_r = jnp.sum(jnp.where(ri == ci, key_c, 0.0), axis=0, keepdims=True)
    remote = jnp.zeros((N, N), F32)
    local_live = []
    for j in range(MAXP):
        tab_r = tab_ref[j : j + 1, :].astype(F32)
        live_r = jnp.where(
            mask_ref[j : j + 1, :] == 1, jnp.clip(length - PAGE * j, 0.0, PAGE), 0.0
        )
        hit = tab_r == rif + PAGE
        req_c += jnp.sum(jnp.where(hit, cif + 1.0, 0.0), axis=1, keepdims=True)
        slot_req_c += jnp.sum(jnp.where(hit, key_r / CH, 0.0), axis=1, keepdims=True)
        nlp_c += jnp.sum(jnp.where(hit, live_r, 0.0), axis=1, keepdims=True)
        local_live.append(column(jnp.where(tab_r < PAGE, live_r, 0.0)))
        remote += jnp.where(column(tab_r) == cif + PAGE, 1.0, 0.0)

    lane = iota((N, 128), 1)
    tsend[...] = jnp.where(
        lane == 0, fetch_c, jnp.where(lane == 1, move_c, jnp.where(lane == 2, nlp_c, 0.0))
    ).astype(I32)

    jj, rr = iota((N, CW), 1), iota((N, CW), 0)
    target = jnp.sum(
        jnp.where(rr == (jj & (N - 1)), key_c, 0.0), axis=0, keepdims=True
    ) + (jj[:1] >> 5).astype(F32)
    place = hot(iota((ROWS, CW), 0).astype(F32) == target)
    cp_hid.wait()
    chunks = jnp.concatenate([hid[:, c * CW : (c + 1) * CW] for c in range(CH)], axis=0)
    hsend[...] = dot(place, chunks).astype(BF)

    blk = 128

    def rows_of(b):
        return pl.ds(pl.multiple_of(b * blk, blk), blk)

    vals = jnp.where(lane == 0, req_c, 0.0)
    for j in range(MAXP):
        vals = jnp.where(lane == j + 1, local_live[j], vals)
    vals = jnp.where(lane == 5, slot_req_c, jnp.where(lane == 6, key_c / CH, vals))
    vals = vals.astype(BF)
    wide = jnp.concatenate([remote] * 4, axis=1)
    for h in range(4):
        mine = (iota((N, 128), 1) >> 5) == h
        mbias[h * N : (h + 1) * N, :] = jnp.where(mine & (wide > 0.0), 0.0, LOW)
    i128, j128 = iota((128, 128), 0), iota((128, 128), 1)
    turn[...] = hot(j128 == ((i128 & 7) << 4) + (((i128 >> 3) & 1) << 3) + (i128 >> 4))

    def build(b, _):
        i = iota((blk, 1), 0) + b * blk
        j = iota((blk, ROWS), 1)
        at = rows_of(b)
        e = hot(iota((blk, N), 1) == (i >> 4))
        ex[at, :] = e
        x = dot(e, vals)
        cx[at, :] = x
        chunk = (i >> 1) & 7
        jf = j.astype(F32)
        wants = x[:, 5:6] * CH + chunk.astype(F32)
        qsel[at, :] = hot(jf == jnp.where(x[:, 0:1] > 0.0, wants, -1.0))
        mine = x[:, 6:7] * CH + chunk.astype(F32)
        qsel[pl.ds(pl.multiple_of(ROWS + b * blk, blk), blk), :] = hot(jf == mine)
        return 0

    lax.fori_loop(0, ROWS // blk, build, 0)

    pl.semaphore_wait(barrier, N - 1 + Z - 1)
    scatter(hsend, hrecv, HEADS, 0)
    scatter(tsend, trecv, 1, 1)
    keep(tsend, trecv, 1)
    keep(hsend, hrecv, HEADS)

    cp_cache.wait()
    small[7].wait()

    def turn_local(r, _):
        for j in range(MAXP):
            page = jnp.minimum(tab_s[j, r], PAGE - 1)
            kt[r, :, j * PAGE : (j + 1) * PAGE] = jnp.transpose(cache[page, 0])
        return 0

    lax.fori_loop(0, N, turn_local, 0, unroll=4)

    cp_down.wait()
    drain(hrecv, HEADS, rsem.at[0])
    arranged = [
        dot(turn[...], hrecv[g * 128 : (g + 1) * 128, :]).astype(BF) for g in range(4)
    ]
    acc = jnp.zeros((2 * N, CW), F32)
    for c in range(CH):
        acc += lax.dot_general(
            jnp.concatenate([x[c * 16 : (c + 1) * 16] for x in arranged], axis=0),
            down[:, c * CW : (c + 1) * CW],
            NT,
            preferred_element_type=F32,
        )
    drain(trecv, 1, rsem.at[1])
    cp_tsm = pltpu.make_async_copy(trecv, tsm, lsem.at[5])
    cp_tsm.start()
    adapter = trecv[:, 0:1].astype(F32)
    adapter = jnp.concatenate(
        [adapter[g * 8 : (g + 1) * 8] for g in (0, 0, 1, 1, 2, 2, 3, 3)], axis=0
    )
    wanted = (iota((2 * N, CW), 1) >> 6).astype(F32) == adapter
    acc = jnp.where(wanted, acc, 0.0)
    acc = acc[:, :128] + acc[:, 128:]
    acc = acc + swap(acc)
    first_half = iota((N, 128), 1) < RANK
    zbuf[pl.ds(z0, 1)] = jnp.where(
        first_half,
        jnp.concatenate([acc[g * 16 : g * 16 + 8] for g in range(4)], axis=0),
        jnp.concatenate([acc[g * 16 + 8 : g * 16 + 16] for g in range(4)], axis=0),
    )[None]
    for k in (2, 1, 3):
        pltpu.make_async_remote_copy(
            src_ref=zbuf.at[z0],
            dst_ref=zbuf.at[z0],
            send_sem=ssem.at[2],
            recv_sem=rsem.at[2],
            device_id={"mp": lax.rem(z0 + k, Z)},
            device_id_type=MESH,
        ).start()
    zpart = zbuf.at[pl.ds(0, Z - 1)]

    cp_tsm.wait()

    def turn_served(d, _):
        kts[d] = jnp.transpose(cache[jnp.clip(tsm[d, 1], 0, PAGE - 1), 0])
        return 0

    lax.fori_loop(0, N, turn_served, 0, unroll=8)
    cp_up.wait()
    pltpu.make_async_copy(zpart, zpart, rsem.at[2]).wait()
    u = (zbuf[0] + zbuf[1]) + (zbuf[2] + zbuf[3])
    turned = swap(u)
    slots = [jnp.where(first_half, u, turned), jnp.where(first_half, turned, u)]
    u = jnp.concatenate([slots[s][g * 8 : (g + 1) * 8] for g in range(4) for s in (0, 1)], axis=0)
    u = jnp.where(wanted, jnp.concatenate([u, u], axis=1), 0.0).astype(BF)
    deltas = [dot(u, up[:, c * CW : (c + 1) * CW]).astype(BF) for c in range(CH)]
    for g in range(4):
        st1[g * 128 : (g + 1) * 128, :] = jnp.concatenate(
            [x[g * 16 : (g + 1) * 16] for x in deltas], axis=0
        )
    for dy in (2, 1, 3, 0):
        at = pl.ds(pl.multiple_of(rows8[dy] * 16, 128), 128)
        dsend[at, :] = dot(turn[...], st1[at, :]).astype(BF)
        peers(dy, sender(dsend, drecv, HEADS, ssem.at[3], rsem.at[3]))
    keep(dsend, drecv, HEADS)

    small[6].wait()
    fresh = fresh_ref[...].reshape(2 * N, CW)
    counts = trecv[...].astype(F32).astype(BF)

    def build_masks(b, _):
        i = iota((blk, 1), 0) + b * blk
        j = iota((blk, ROWS), 1)
        t = iota((blk, PAGE), 1).astype(F32)
        at = rows_of(b)
        ph[at, :] = hot(j == ((i & 31) << 4) + (i >> 5))
        n_live = dot(ex[at, :], counts)[:, 2:3]
        sbias[at, :] = jnp.where(t < n_live, 0.0, LOW)
        x = cx[at, :]
        for k in range(MAXP):
            lbias[at, k * PAGE : (k + 1) * PAGE] = jnp.where(t < x[:, k + 1 : k + 2], 0.0, LOW)
        k0 = dot(hot(iota((blk, 2 * N), 1) == (i >> 4) * 2), fresh)
        v0 = dot(hot(iota((blk, 2 * N), 1) == (i >> 4) * 2 + 1), fresh)
        fkv[at, :] = jnp.concatenate(
            [
                block_select(k0[:, :HD], k0[:, HD:], blk),
                block_select(v0[:, :HD], v0[:, HD:], blk),
            ],
            axis=1,
        )
        return 0

    lax.fori_loop(0, ROWS // blk, build_masks, 0)
    cp_base.wait()
    chunked = jnp.concatenate([base[:, c * CW : (c + 1) * CW] for c in range(CH)], axis=0)

    def build_base(b, _):
        i = iota((blk, 1), 0) + b * blk
        j = iota((blk, CW), 1)
        at = rows_of(b)
        head = ((i >> 1) & 7) << 5
        req = cx[at, 0:1]
        want = jnp.where(req > 0.0, req - 1.0 + head.astype(F32), -1.0)
        both = dot(hot(j.astype(F32) == want), chunked)
        basep[at, :] = jnp.where((i & 1) == 0, both[:, :HD], both[:, HD:])
        both = dot(hot(j == head + (i >> 4)), chunked)
        basel[at, :] = jnp.where((i & 1) == 0, both[:, :HD], both[:, HD:])
        return 0

    lax.fori_loop(0, ROWS // blk, build_base, 0)
    odd = (iota((128, 1), 0) & 1) == 1
    halves = iota((HEADS, CW), 1) >> 7
    heads_of = hot(halves == ((iota((HEADS, CW), 0) >> 3) & 1))

    drain(drecv, HEADS, rsem.at[3])

    def pick(selector, base_rows):
        both = dot(selector, drecv[...])
        return (base_rows + 2.0 * jnp.where(odd, both[:, HD:], both[:, :HD])).astype(BF)

    for dy in (2, 1, 3, 0):
        at = pl.ds(pl.multiple_of(rows8[dy] * 16, 128), 128)
        qsend[at, :] = pick(qsel[at, :], basep[at, :])
        peers(dy, sender(qsend, qrecv, HEADS, ssem.at[4], None, gsem))
    keep(qsend, qrecv, HEADS)

    def spread_heads(q):
        return jnp.concatenate([q, q], axis=1) * jnp.concatenate([heads_of] * (q.shape[0] // HEADS), axis=0)

    for b in range(ROWS // 128):
        at = slice(b * 128, (b + 1) * 128)
        mine = pick(qsel[ROWS + b * 128 : ROWS + (b + 1) * 128, :], basel[at, :])
        qbd[at, :] = spread_heads(mine)
        loc[at, 0:1] = jnp.sum(mine.astype(F32) * fkv[at, :HD], axis=1, keepdims=True) * SCALE

    def local_scores(r, _):
        at = pl.ds(pl.multiple_of(r * HEADS, HEADS), HEADS)
        sl[at, :] = dot(qbd[at, :], kt[r])
        return 0


    def local_weights(b):
        at = slice(b * 256, (b + 1) * 256)
        new = loc[at, 0:1]
        parts = [
            sl[at, j * PAGE : (j + 1) * PAGE] * SCALE + lbias[at, j * PAGE : (j + 1) * PAGE]
            for j in range(MAXP)
        ]
        m = jnp.maximum(jnp.maximum(parts[0], parts[1]), jnp.maximum(parts[2], parts[3]))
        m = jnp.maximum(jnp.max(m, axis=1, keepdims=True), new)
        wf = jnp.exp(new - m)
        total = jnp.zeros((256, PAGE), F32)
        for j in range(MAXP):
            w = jnp.exp(parts[j] - m)
            total += w
            wl[at, j * PAGE : (j + 1) * PAGE] = w.astype(BF)
        total = jnp.sum(total, axis=1, keepdims=True) + wf
        at_lane = iota((256, 128), 1)
        stat = jnp.where(at_lane == 0, m, jnp.where(at_lane == 1, total, 0.0))
        loc[at, :] = jnp.where(at_lane == 2, wf, stat)

    def serve(*hops):
        slots = [d0] if 0 in hops else []
        for dist in hops:
            near = [
                rows8[dy] + around[dx][dc]
                for dy in range(4)
                for dx in range(4)
                for dc in range(2)
                if FAR[dy] + FAR[dx] == dist and (dy, dx, dc) != (0, 0, 0)
            ]
            drain(qrecv, HEADS, gsem.at[dist], len(near))
            slots += near
        n = len(slots) * HEADS
        ats = [pl.ds(pl.multiple_of(slot * HEADS, HEADS), HEADS) for slot in slots]
        s = [dot(spread_heads(qrecv[at, :]), kts[slot]) for at, slot in zip(ats, slots)]
        bias = jnp.concatenate([sbias[at, :] for at in ats], axis=0)
        s = jnp.concatenate(s, axis=0) * SCALE + bias
        m = jnp.max(s, axis=1, keepdims=True)
        w = jnp.exp(s - m)
        total = jnp.sum(w, axis=1, keepdims=True)
        w = w.astype(BF)
        o = [
            dot(
                w[i * HEADS : (i + 1) * HEADS],
                cache[jnp.clip(tsm[slot, 1], 0, PAGE - 1), 1],
            )
            for i, slot in enumerate(slots)
        ]
        o = jnp.concatenate(o, axis=0)
        o = (block_select(o[:, :HD], o[:, HD:], n) / total).astype(BF)
        lse = jnp.where(
            iota((n, 128), 1) == (iota((n, 128), 0) & 15), m + jnp.log(total), 0.0
        )
        lse = jnp.sum(lse.reshape(n // HEADS, HEADS, 128), axis=1)
        for i, slot in enumerate(slots):
            lsend[pl.ds(slot, 1), :] = lse[i : i + 1]
            psend[ats[i], :] = o[i * HEADS : (i + 1) * HEADS]
        for slot in slots[1 if 0 in hops else 0 :]:
            sender(lsend, lrecv, 1, ssem.at[6], rsem.at[6])(slot, None)
            sender(psend, precv, HEADS, ssem.at[5], rsem.at[5])(slot, None)

    lax.fori_loop(0, N // 2, local_scores, 0, unroll=8)
    serve(0, 1, 2)
    serve(4)
    serve(3)
    keep(lsend, lrecv, 1)
    keep(psend, precv, HEADS)

    lax.fori_loop(N // 2, N, local_scores, 0, unroll=8)
    local_weights(0)
    local_weights(1)

    def local_values(r, _):
        at = pl.ds(pl.multiple_of(r * HEADS, HEADS), HEADS)
        o = jnp.zeros((HEADS, CW), F32)
        for j in range(MAXP):
            page = jnp.minimum(tab_s[j, r], PAGE - 1)
            o += dot(wl[at, j * PAGE : (j + 1) * PAGE], cache[page, 1])
        ol[at, :] = block_select(o[:, :HD], o[:, HD:], HEADS)
        return 0

    lax.fori_loop(0, N, local_values, 0, unroll=8)

    def local_part(b, _):
        at = rows_of(b)
        st = loc[at, :]
        m, total, wf = st[:, 0:1], st[:, 1:2], st[:, 2:3].astype(BF).astype(F32)
        o = (ol[at, :] + wf * fkv[at, HD:]) / total
        hi, mid, lo = pieces(m + jnp.log(total))
        at_lane = iota((blk, 128), 1)
        stat = jnp.where(at_lane == 0, hi, jnp.where(at_lane == 1, mid, 0.0))
        stat = jnp.where(at_lane == 2, lo, stat)
        locp[at, :HD] = o.astype(BF)
        locp[at, HD:] = stat.astype(BF)
        return 0

    lax.fori_loop(0, ROWS // blk, local_part, 0, unroll=4)
    mine = dot(ph[...], locp[...])
    ol[...] = mine[:, :HD]
    loc[...] = jnp.broadcast_to(
        mine[:, HD : HD + 1] + mine[:, HD + 1 : HD + 2] + mine[:, HD + 2 : HD + 3], (ROWS, 128)
    )

    drain(lrecv, 1, rsem.at[6])
    stats = jnp.transpose(lrecv[...])
    drain(precv, HEADS, rsem.at[5])
    others = dot(ph[...], precv[...]).astype(BF)
    others = jnp.concatenate([others, jnp.ones((ROWS, 128), BF)], axis=1)
    for g in range(4):
        at = slice(g * 128, (g + 1) * 128)
        row = jnp.concatenate([stats[4 * g + i : 4 * g + i + 1, :] for i in range(4)], axis=1)
        lse = row + mbias[...]
        mine = loc[at, :]
        top = jnp.maximum(jnp.max(lse, axis=1, keepdims=True), mine)
        both = dot(jnp.exp(lse - top).astype(BF), others[at])
        wm = jnp.exp(mine - top)
        o = (both[:, :HD] + wm * ol[at, :]) / (both[:, HD:] + wm)
        for i in range(4):
            h = 4 * g + i
            out_ref[:, h * HD : (h + 1) * HD] = o[i * N : (i + 1) * N].astype(BF)

    drain(hsend, HEADS, ssem.at[0])
    drain(tsend, 1, ssem.at[1])
    pltpu.make_async_copy(zpart, zpart, ssem.at[2]).wait()
    drain(dsend, HEADS, ssem.at[3])
    drain(qsend, HEADS, ssem.at[4])
    drain(psend, HEADS, ssem.at[5])
    drain(lsend, 1, ssem.at[6])


def shards(
    hidden,
    base_query_projection,
    adapter_owner_map,
    adapter_fetch_table,
    adapter_down_panels,
    adapter_up_panels,
    key_value_page_cache,
    request_page_table,
    page_transfer_table,
    page_entry_mask,
    lengths,
    fresh_key_value,
):
    width = N * 64
    table = request_page_table.T
    vmem = pl.BlockSpec(memory_space=pltpu.VMEM)
    hbm = pl.BlockSpec(memory_space=pltpu.HBM)
    v = pltpu.VMEM
    return pl.pallas_call(
        kernel,
        out_shape=jax.ShapeDtypeStruct((N, width), BF),
        in_specs=[hbm] * 12,
        out_specs=vmem,
        scratch_shapes=[
            v((1, N), I32),
            v((1, N), I32),
            v((MAXP, N), I32),
            v((1, N), I32),
            v((MAXP, N), I32),
            v((1, N), I32),
            v((N, 2, CW), BF),
            pltpu.SMEM((MAXP, N), I32),
            v((N, width), BF),
            v((N, width), BF),
            v((CW, width), BF),
            v((CW, width), BF),
            v((PAGE, 2, PAGE, CW), BF),
            v((N, CW, MAXP * PAGE), BF),
            v((N, CW, PAGE), BF),
            v((ROWS, CW), BF),
            v((ROWS, CW), BF),
            v((ROWS, CW), BF),
            v((ROWS, CW), BF),
            v((N, 128), I32),
            v((N, 128), I32),
            pltpu.SMEM((N, 128), I32),
            v((Z, N, 128), F32),
            v((ROWS, HD), BF),
            v((ROWS, HD), BF),
            v((ROWS, HD), BF),
            v((ROWS, HD), BF),
            v((N, 128), F32),
            v((N, 128), F32),
            v((128, 128), BF),
            v((ROWS, ROWS), BF),
            v((2 * ROWS, ROWS), BF),
            v((ROWS, N), BF),
            v((ROWS, 128), F32),
            v((ROWS, CW), BF),
            v((ROWS, HD), F32),
            v((ROWS, HD), F32),
            v((ROWS, CW), BF),
            v((ROWS, CW), F32),
            v((ROWS, ROWS), F32),
            v((ROWS, ROWS), BF),
            v((ROWS, ROWS), F32),
            v((ROWS, PAGE), F32),
            v((128, 128), F32),
            v((ROWS, HD), F32),
            v((ROWS, 128), F32),
            v((ROWS, CW), BF),
            pltpu.SemaphoreType.DMA((14,)),
            pltpu.SemaphoreType.DMA((7,)),
            pltpu.SemaphoreType.DMA((7,)),
            pltpu.SemaphoreType.DMA((5,)),
        ],
        compiler_params=pltpu.CompilerParams(
            collective_id=0, has_side_effects=True, vmem_limit_bytes=63 * 1024 * 1024
        ),
    )(
        adapter_owner_map.T,
        adapter_fetch_table,
        table,
        page_transfer_table,
        page_entry_mask.T,
        lengths.reshape(1, N),
        fresh_key_value,
        hidden,
        base_query_projection,
        adapter_down_panels.reshape(CW, width),
        adapter_up_panels.reshape(CW, width),
        key_value_page_cache,
    )


def solution(mesh):
    return jax.shard_map(
        shards,
        mesh=mesh,
        in_specs=(
            P("dp", "mp"),
            P("dp", "mp"),
            P("dp", None),
            P("dp", None),
            P("dp", None, "mp"),
            P("dp", None, "mp"),
            P("dp", None, None, "mp"),
            P("dp", None),
            P("dp", None),
            P("dp", None),
            P("dp"),
            P("dp", None, "mp"),
        ),
        out_specs=P("dp", "mp"),
        check_vma=False,
    )
```

```python
import functools
import math

import jax
import jax.numpy as jnp
from jax import lax
from jax.experimental import pallas as pl
from jax.experimental.pallas import tpu as pltpu
from jax.sharding import PartitionSpec as P

MESH = pl.DeviceIdType.MESH
BF, F32, I32 = jnp.bfloat16, jnp.float32, jnp.int32

N = 32
Z = 4
HD = 128
HEADS = 16
PAGE = 128
MAXP = 4
RANK = 64
CH = 8
CW = 256
ROWS = N * HEADS
FAR = (0, 1, 2, 1)
SCALE = 1.0 / math.sqrt(HD)
LOW = -1e30
NT = (((1,), (1,)), ((), ()))


def iota(shape, dim):
    return lax.broadcasted_iota(I32, shape, dim)


def hot(mask):
    return jnp.where(mask, 1.0, 0.0).astype(BF)


def dot(a, b):
    return jnp.dot(a, b, preferred_element_type=F32)


def pieces(x):
    hi = x.astype(BF).astype(F32)
    mid = (x - hi).astype(BF).astype(F32)
    return hi, mid, x - hi - mid


def swap(x):
    return jnp.concatenate([x[:, RANK:], x[:, :RANK]], axis=1)


def block_select(left, right, rows):
    low_heads = (iota((rows, 1), 0) & 8) == 0
    return jnp.where(low_heads, left, right)


def kernel(
    own_hbm, fetch_hbm, tab_hbm, move_hbm, mask_hbm, len_hbm, fresh_hbm,
    hid_hbm, base_hbm, down_hbm, up_hbm, cache_hbm,
    out_ref,
    own_ref, fetch_ref, tab_ref, move_ref, mask_ref, len_ref, fresh_ref, tab_s,
    outv, hid, base, down, up, cache, kt, kts,
    hsend, hrecv, dsend, drecv, tsend, trecv, tsm, zbuf,
    qsend, qrecv, psend, precv, lsend, lrecv,
    turn, ph, qsel, ex, cx, st1, basep, basel,
    qbd, fkv, sl, wl, lbias, sbias, mbias, ol, loc, locp,
    lsem, ssem, rsem, gsem,
):
    d0 = lax.axis_index("dp")
    z0 = lax.axis_index("mp")
    y0, x0, c0 = lax.div(d0, 8), lax.rem(lax.div(d0, 2), 4), lax.rem(d0, 2)
    rows8 = [lax.rem(y0 + dy, 4) * 8 for dy in range(4)]
    around = [[lax.rem(x0 + dx, 4) * 2 + c for c in (c0, 1 - c0)] for dx in range(4)]

    barrier = pltpu.get_barrier_semaphore()

    def peers(dy, visit):
        for dx in (2, 1, 3, 0):
            for dc in (1, 0):
                if (dy, dx, dc) != (0, 0, 0):
                    visit(rows8[dy] + around[dx][dc], FAR[dy] + FAR[dx])

    def greet(t, _):
        pl.semaphore_signal(barrier, inc=1, device_id={"dp": t}, device_id_type=MESH)

    for dy in (2, 1, 3, 0):
        peers(dy, greet)
    for k in range(1, Z):
        pl.semaphore_signal(
            barrier, inc=1, device_id={"mp": lax.rem(z0 + k, Z)}, device_id_type=MESH
        )

    cp_hid = pltpu.make_async_copy(hid_hbm, hid, lsem.at[0])
    cp_base = pltpu.make_async_copy(base_hbm, base, lsem.at[1])
    cp_down = pltpu.make_async_copy(down_hbm, down, lsem.at[2])
    cp_up = pltpu.make_async_copy(up_hbm, up, lsem.at[3])
    cp_cache = pltpu.make_async_copy(cache_hbm, cache, lsem.at[4])
    small = [
        pltpu.make_async_copy(src, dst, lsem.at[6 + i])
        for i, (src, dst) in enumerate((
            (own_hbm, own_ref), (fetch_hbm, fetch_ref), (tab_hbm, tab_ref),
            (move_hbm, move_ref), (mask_hbm, mask_ref), (len_hbm, len_ref),
            (fresh_hbm, fresh_ref), (tab_hbm, tab_s),
        ))
    ]
    for cp in (*small, cp_hid, cp_down, cp_up, cp_base, cp_cache):
        cp.start()

    def sender(src, dst, rows, send_sem, recv_sem, per_hops=None):
        def visit(t, hops):
            pltpu.make_async_remote_copy(
                src_ref=src.at[pl.ds(pl.multiple_of(t * rows, rows), rows)],
                dst_ref=dst.at[pl.ds(pl.multiple_of(d0 * rows, rows), rows)],
                send_sem=send_sem,
                recv_sem=recv_sem if per_hops is None else per_hops.at[hops],
                device_id={"dp": t},
                device_id_type=MESH,
            ).start()

        return visit

    def scatter(src, dst, rows, which):
        for dy in (2, 1, 3, 0):
            peers(dy, sender(src, dst, rows, ssem.at[which], rsem.at[which]))

    def drain(ref, rows, sem, count=N - 1):
        part = ref.at[pl.ds(0, count * rows)]
        pltpu.make_async_copy(part, part, sem).wait()

    def keep(src, dst, rows):
        here = pl.ds(pl.multiple_of(d0 * rows, rows), rows)
        dst[here, :] = src[here, :]

    ri, ci = iota((N, N), 0), iota((N, N), 1)
    rif, cif = ri.astype(F32), ci.astype(F32)

    def column(row):
        return jnp.sum(jnp.where(ri == ci, row, 0.0), axis=1, keepdims=True)

    for cp in small[:6]:
        cp.wait()
    own_r = own_ref[...].astype(F32)
    own_c = column(own_r)
    same = own_c == own_r
    rank_c = jnp.sum(jnp.where(same & (ci < ri), 1.0, 0.0), axis=1, keepdims=True)
    key_c = own_c * HEADS + rank_c * CH
    length = len_ref[...].astype(F32)
    fetch_c = column(fetch_ref[...].astype(F32))
    move_c = column(move_ref[...].astype(F32))
    req_c = jnp.zeros((N, 1), F32)
    nlp_c = jnp.zeros((N, 1), F32)
    slot_req_c = jnp.zeros((N, 1), F32)
    key_r = jnp.sum(jnp.where(ri == ci, key_c, 0.0), axis=0, keepdims=True)
    remote = jnp.zeros((N, N), F32)
    local_live = []
    for j in range(MAXP):
        tab_r = tab_ref[j : j + 1, :].astype(F32)
        live_r = jnp.where(
            mask_ref[j : j + 1, :] == 1, jnp.clip(length - PAGE * j, 0.0, PAGE), 0.0
        )
        hit = tab_r == rif + PAGE
        req_c += jnp.sum(jnp.where(hit, cif + 1.0, 0.0), axis=1, keepdims=True)
        slot_req_c += jnp.sum(jnp.where(hit, key_r / CH, 0.0), axis=1, keepdims=True)
        nlp_c += jnp.sum(jnp.where(hit, live_r, 0.0), axis=1, keepdims=True)
        local_live.append(column(jnp.where(tab_r < PAGE, live_r, 0.0)))
        remote += jnp.where(column(tab_r) == cif + PAGE, 1.0, 0.0)

    lane = iota((N, 128), 1)
    tsend[...] = jnp.where(
        lane == 0, fetch_c, jnp.where(lane == 1, move_c, jnp.where(lane == 2, nlp_c, 0.0))
    ).astype(I32)

    jj, rr = iota((N, CW), 1), iota((N, CW), 0)
    target = jnp.sum(
        jnp.where(rr == (jj & (N - 1)), key_c, 0.0), axis=0, keepdims=True
    ) + (jj[:1] >> 5).astype(F32)
    place = hot(iota((ROWS, CW), 0).astype(F32) == target)
    cp_hid.wait()
    chunks = jnp.concatenate([hid[:, c * CW : (c + 1) * CW] for c in range(CH)], axis=0)
    hsend[...] = dot(place, chunks).astype(BF)

    blk = 128

    def rows_of(b):
        return pl.ds(pl.multiple_of(b * blk, blk), blk)

    vals = jnp.where(lane == 0, req_c, 0.0)
    for j in range(MAXP):
        vals = jnp.where(lane == j + 1, local_live[j], vals)
    vals = jnp.where(lane == 5, slot_req_c, jnp.where(lane == 6, key_c / CH, vals))
    vals = vals.astype(BF)
    wide = jnp.concatenate([remote] * 4, axis=1)
    for h in range(4):
        mine = (iota((N, 128), 1) >> 5) == h
        mbias[h * N : (h + 1) * N, :] = jnp.where(mine & (wide > 0.0), 0.0, LOW)
    i128, j128 = iota((128, 128), 0), iota((128, 128), 1)
    turn[...] = hot(j128 == ((i128 & 7) << 4) + (((i128 >> 3) & 1) << 3) + (i128 >> 4))

    def build(b, _):
        i = iota((blk, 1), 0) + b * blk
        j = iota((blk, ROWS), 1)
        at = rows_of(b)
        e = hot(iota((blk, N), 1) == (i >> 4))
        ex[at, :] = e
        x = dot(e, vals)
        cx[at, :] = x
        chunk = (i >> 1) & 7
        jf = j.astype(F32)
        wants = x[:, 5:6] * CH + chunk.astype(F32)
        qsel[at, :] = hot(jf == jnp.where(x[:, 0:1] > 0.0, wants, -1.0))
        mine = x[:, 6:7] * CH + chunk.astype(F32)
        qsel[pl.ds(pl.multiple_of(ROWS + b * blk, blk), blk), :] = hot(jf == mine)
        return 0

    lax.fori_loop(0, ROWS // blk, build, 0)

    pl.semaphore_wait(barrier, N - 1 + Z - 1)
    scatter(hsend, hrecv, HEADS, 0)
    scatter(tsend, trecv, 1, 1)
    keep(tsend, trecv, 1)
    keep(hsend, hrecv, HEADS)

    cp_cache.wait()
    small[7].wait()

    def turn_local(r, _):
        for j in range(MAXP):
            page = jnp.minimum(tab_s[j, r], PAGE - 1)
            kt[r, :, j * PAGE : (j + 1) * PAGE] = jnp.transpose(cache[page, 0])
        return 0

    lax.fori_loop(0, N, turn_local, 0, unroll=4)

    cp_down.wait()
    drain(hrecv, HEADS, rsem.at[0])
    arranged = [
        dot(turn[...], hrecv[g * 128 : (g + 1) * 128, :]).astype(BF) for g in range(4)
    ]
    acc = jnp.zeros((2 * N, CW), F32)
    for c in range(CH):
        acc += lax.dot_general(
            jnp.concatenate([x[c * 16 : (c + 1) * 16] for x in arranged], axis=0),
            down[:, c * CW : (c + 1) * CW],
            NT,
            preferred_element_type=F32,
        )
    drain(trecv, 1, rsem.at[1])
    cp_tsm = pltpu.make_async_copy(trecv, tsm, lsem.at[5])
    cp_tsm.start()
    adapter = trecv[:, 0:1].astype(F32)
    adapter = jnp.concatenate(
        [adapter[g * 8 : (g + 1) * 8] for g in (0, 0, 1, 1, 2, 2, 3, 3)], axis=0
    )
    wanted = (iota((2 * N, CW), 1) >> 6).astype(F32) == adapter
    acc = jnp.where(wanted, acc, 0.0)
    acc = acc[:, :128] + acc[:, 128:]
    acc = acc + swap(acc)
    first_half = iota((N, 128), 1) < RANK
    zbuf[pl.ds(z0, 1)] = jnp.where(
        first_half,
        jnp.concatenate([acc[g * 16 : g * 16 + 8] for g in range(4)], axis=0),
        jnp.concatenate([acc[g * 16 + 8 : g * 16 + 16] for g in range(4)], axis=0),
    )[None]
    for k in (2, 1, 3):
        pltpu.make_async_remote_copy(
            src_ref=zbuf.at[z0],
            dst_ref=zbuf.at[z0],
            send_sem=ssem.at[2],
            recv_sem=rsem.at[2],
            device_id={"mp": lax.rem(z0 + k, Z)},
            device_id_type=MESH,
        ).start()
    zpart = zbuf.at[pl.ds(0, Z - 1)]

    cp_tsm.wait()

    def turn_served(d, _):
        kts[d] = jnp.transpose(cache[jnp.clip(tsm[d, 1], 0, PAGE - 1), 0])
        return 0

    lax.fori_loop(0, N, turn_served, 0, unroll=8)
    cp_up.wait()
    pltpu.make_async_copy(zpart, zpart, rsem.at[2]).wait()
    u = (zbuf[0] + zbuf[1]) + (zbuf[2] + zbuf[3])
    turned = swap(u)
    slots = [jnp.where(first_half, u, turned), jnp.where(first_half, turned, u)]
    u = jnp.concatenate([slots[s][g * 8 : (g + 1) * 8] for g in range(4) for s in (0, 1)], axis=0)
    u = jnp.where(wanted, jnp.concatenate([u, u], axis=1), 0.0).astype(BF)
    deltas = [dot(u, up[:, c * CW : (c + 1) * CW]).astype(BF) for c in range(CH)]
    for g in range(4):
        st1[g * 128 : (g + 1) * 128, :] = jnp.concatenate(
            [x[g * 16 : (g + 1) * 16] for x in deltas], axis=0
        )
    for dy in (2, 1, 3, 0):
        at = pl.ds(pl.multiple_of(rows8[dy] * 16, 128), 128)
        dsend[at, :] = dot(turn[...], st1[at, :]).astype(BF)
        peers(dy, sender(dsend, drecv, HEADS, ssem.at[3], rsem.at[3]))
    keep(dsend, drecv, HEADS)

    small[6].wait()
    fresh = fresh_ref[...].reshape(2 * N, CW)
    counts = trecv[...].astype(F32).astype(BF)

    def build_masks(b, _):
        i = iota((blk, 1), 0) + b * blk
        j = iota((blk, ROWS), 1)
        t = iota((blk, PAGE), 1).astype(F32)
        at = rows_of(b)
        ph[at, :] = hot(j == ((i & 31) << 4) + (i >> 5))
        n_live = dot(ex[at, :], counts)[:, 2:3]
        sbias[at, :] = jnp.where(t < n_live, 0.0, LOW)
        x = cx[at, :]
        for k in range(MAXP):
            lbias[at, k * PAGE : (k + 1) * PAGE] = jnp.where(t < x[:, k + 1 : k + 2], 0.0, LOW)
        k0 = dot(hot(iota((blk, 2 * N), 1) == (i >> 4) * 2), fresh)
        v0 = dot(hot(iota((blk, 2 * N), 1) == (i >> 4) * 2 + 1), fresh)
        fkv[at, :] = jnp.concatenate(
            [
                block_select(k0[:, :HD], k0[:, HD:], blk),
                block_select(v0[:, :HD], v0[:, HD:], blk),
            ],
            axis=1,
        )
        return 0

    lax.fori_loop(0, ROWS // blk, build_masks, 0)
    cp_base.wait()
    chunked = jnp.concatenate([base[:, c * CW : (c + 1) * CW] for c in range(CH)], axis=0)

    def build_base(b, _):
        i = iota((blk, 1), 0) + b * blk
        j = iota((blk, CW), 1)
        at = rows_of(b)
        head = ((i >> 1) & 7) << 5
        req = cx[at, 0:1]
        want = jnp.where(req > 0.0, req - 1.0 + head.astype(F32), -1.0)
        both = dot(hot(j.astype(F32) == want), chunked)
        basep[at, :] = jnp.where((i & 1) == 0, both[:, :HD], both[:, HD:])
        both = dot(hot(j == head + (i >> 4)), chunked)
        basel[at, :] = jnp.where((i & 1) == 0, both[:, :HD], both[:, HD:])
        return 0

    lax.fori_loop(0, ROWS // blk, build_base, 0)
    odd = (iota((128, 1), 0) & 1) == 1
    halves = iota((HEADS, CW), 1) >> 7
    heads_of = hot(halves == ((iota((HEADS, CW), 0) >> 3) & 1))

    drain(drecv, HEADS, rsem.at[3])

    def pick(selector, base_rows):
        both = dot(selector, drecv[...])
        return (base_rows + 2.0 * jnp.where(odd, both[:, HD:], both[:, :HD])).astype(BF)

    for dy in (2, 1, 3, 0):
        at = pl.ds(pl.multiple_of(rows8[dy] * 16, 128), 128)
        qsend[at, :] = pick(qsel[at, :], basep[at, :])
        peers(dy, sender(qsend, qrecv, HEADS, ssem.at[4], None, gsem))
    keep(qsend, qrecv, HEADS)

    def spread_heads(q):
        return jnp.concatenate([q, q], axis=1) * jnp.concatenate([heads_of] * (q.shape[0] // HEADS), axis=0)

    for b in range(ROWS // 128):
        at = slice(b * 128, (b + 1) * 128)
        mine = pick(qsel[ROWS + b * 128 : ROWS + (b + 1) * 128, :], basel[at, :])
        qbd[at, :] = spread_heads(mine)
        loc[at, 0:1] = jnp.sum(mine.astype(F32) * fkv[at, :HD], axis=1, keepdims=True) * SCALE

    def local_scores(r, _):
        at = pl.ds(pl.multiple_of(r * HEADS, HEADS), HEADS)
        sl[at, :] = dot(qbd[at, :], kt[r])
        return 0


    def local_weights(b):
        at = slice(b * 256, (b + 1) * 256)
        new = loc[at, 0:1]
        parts = [
            sl[at, j * PAGE : (j + 1) * PAGE] * SCALE + lbias[at, j * PAGE : (j + 1) * PAGE]
            for j in range(MAXP)
        ]
        m = jnp.maximum(jnp.maximum(parts[0], parts[1]), jnp.maximum(parts[2], parts[3]))
        m = jnp.maximum(jnp.max(m, axis=1, keepdims=True), new)
        wf = jnp.exp(new - m)
        total = jnp.zeros((256, PAGE), F32)
        for j in range(MAXP):
            w = jnp.exp(parts[j] - m)
            total += w
            wl[at, j * PAGE : (j + 1) * PAGE] = w.astype(BF)
        total = jnp.sum(total, axis=1, keepdims=True) + wf
        at_lane = iota((256, 128), 1)
        stat = jnp.where(at_lane == 0, m, jnp.where(at_lane == 1, total, 0.0))
        loc[at, :] = jnp.where(at_lane == 2, wf, stat)

    def serve(*hops):
        slots = [d0] if 0 in hops else []
        for dist in hops:
            near = [
                rows8[dy] + around[dx][dc]
                for dy in range(4)
                for dx in range(4)
                for dc in range(2)
                if FAR[dy] + FAR[dx] == dist and (dy, dx, dc) != (0, 0, 0)
            ]
            drain(qrecv, HEADS, gsem.at[dist], len(near))
            slots += near
        n = len(slots) * HEADS
        ats = [pl.ds(pl.multiple_of(slot * HEADS, HEADS), HEADS) for slot in slots]
        s = [dot(spread_heads(qrecv[at, :]), kts[slot]) for at, slot in zip(ats, slots)]
        bias = jnp.concatenate([sbias[at, :] for at in ats], axis=0)
        s = jnp.concatenate(s, axis=0) * SCALE + bias
        m = jnp.max(s, axis=1, keepdims=True)
        w = jnp.exp(s - m)
        total = jnp.sum(w, axis=1, keepdims=True)
        w = w.astype(BF)
        o = [
            dot(
                w[i * HEADS : (i + 1) * HEADS],
                cache[jnp.clip(tsm[slot, 1], 0, PAGE - 1), 1],
            )
            for i, slot in enumerate(slots)
        ]
        o = jnp.concatenate(o, axis=0)
        o = (block_select(o[:, :HD], o[:, HD:], n) / total).astype(BF)
        lse = jnp.where(
            iota((n, 128), 1) == (iota((n, 128), 0) & 15), m + jnp.log(total), 0.0
        )
        lse = jnp.sum(lse.reshape(n // HEADS, HEADS, 128), axis=1)
        for i, slot in enumerate(slots):
            lsend[pl.ds(slot, 1), :] = lse[i : i + 1]
            psend[ats[i], :] = o[i * HEADS : (i + 1) * HEADS]
        for slot in slots[1 if 0 in hops else 0 :]:
            sender(lsend, lrecv, 1, ssem.at[6], rsem.at[6])(slot, None)
            sender(psend, precv, HEADS, ssem.at[5], rsem.at[5])(slot, None)

    lax.fori_loop(0, N // 2, local_scores, 0, unroll=8)
    serve(0, 1, 2)
    serve(4)
    serve(3)
    keep(lsend, lrecv, 1)
    keep(psend, precv, HEADS)

    lax.fori_loop(N // 2, N, local_scores, 0, unroll=8)
    local_weights(0)
    local_weights(1)

    def local_values(r, _):
        at = pl.ds(pl.multiple_of(r * HEADS, HEADS), HEADS)
        o = jnp.zeros((HEADS, CW), F32)
        for j in range(MAXP):
            page = jnp.minimum(tab_s[j, r], PAGE - 1)
            o += dot(wl[at, j * PAGE : (j + 1) * PAGE], cache[page, 1])
        ol[at, :] = block_select(o[:, :HD], o[:, HD:], HEADS)
        return 0

    lax.fori_loop(0, N, local_values, 0, unroll=8)

    def local_part(b, _):
        at = rows_of(b)
        st = loc[at, :]
        m, total, wf = st[:, 0:1], st[:, 1:2], st[:, 2:3].astype(BF).astype(F32)
        o = (ol[at, :] + wf * fkv[at, HD:]) / total
        hi, mid, lo = pieces(m + jnp.log(total))
        at_lane = iota((blk, 128), 1)
        stat = jnp.where(at_lane == 0, hi, jnp.where(at_lane == 1, mid, 0.0))
        stat = jnp.where(at_lane == 2, lo, stat)
        locp[at, :HD] = o.astype(BF)
        locp[at, HD:] = stat.astype(BF)
        return 0

    lax.fori_loop(0, ROWS // blk, local_part, 0, unroll=4)
    mine = dot(ph[...], locp[...])
    ol[...] = mine[:, :HD]
    loc[...] = jnp.broadcast_to(
        mine[:, HD : HD + 1] + mine[:, HD + 1 : HD + 2] + mine[:, HD + 2 : HD + 3], (ROWS, 128)
    )

    drain(lrecv, 1, rsem.at[6])
    stats = jnp.transpose(lrecv[...])
    shares = []
    for g in range(4):
        mine = loc[g * 128 : (g + 1) * 128, :]
        row = jnp.concatenate([stats[4 * g + i : 4 * g + i + 1, :] for i in range(4)], axis=1)
        lse = row + mbias[...]
        top = jnp.maximum(jnp.max(lse, axis=1, keepdims=True), mine)
        shares.append((jnp.exp(lse - top).astype(BF), jnp.exp(mine - top)))
    drain(precv, HEADS, rsem.at[5])
    others = dot(ph[...], precv[...]).astype(BF)
    others = jnp.concatenate([others, jnp.ones((ROWS, 128), BF)], axis=1)
    results = []
    for g, (w, wm) in enumerate(shares):
        at = slice(g * 128, (g + 1) * 128)
        both = dot(w, others[at])
        o = (both[:, :HD] + wm * ol[at, :]) / (both[:, HD:] + wm)
        for i in range(4):
            h = 4 * g + i
            outv[:, h * HD : (h + 1) * HD] = o[i * N : (i + 1) * N].astype(BF)
        part = pl.ds(g * 4 * HD, 4 * HD)
        results.append(pltpu.make_async_copy(outv.at[:, part], out_ref.at[:, part], lsem.at[14 + g]))
        results[-1].start()

    drain(hsend, HEADS, ssem.at[0])
    drain(tsend, 1, ssem.at[1])
    pltpu.make_async_copy(zpart, zpart, ssem.at[2]).wait()
    drain(dsend, HEADS, ssem.at[3])
    drain(qsend, HEADS, ssem.at[4])
    drain(psend, HEADS, ssem.at[5])
    drain(lsend, 1, ssem.at[6])
    for cp in results:
        cp.wait()


def shards(
    hidden,
    base_query_projection,
    adapter_owner_map,
    adapter_fetch_table,
    adapter_down_panels,
    adapter_up_panels,
    key_value_page_cache,
    request_page_table,
    page_transfer_table,
    page_entry_mask,
    lengths,
    fresh_key_value,
):
    width = N * 64
    table = request_page_table.T
    hbm = pl.BlockSpec(memory_space=pltpu.HBM)
    v = pltpu.VMEM
    return pl.pallas_call(
        kernel,
        out_shape=jax.ShapeDtypeStruct((N, width), BF),
        in_specs=[hbm] * 12,
        out_specs=hbm,
        scratch_shapes=[
            v((1, N), I32),
            v((1, N), I32),
            v((MAXP, N), I32),
            v((1, N), I32),
            v((MAXP, N), I32),
            v((1, N), I32),
            v((N, 2, CW), BF),
            pltpu.SMEM((MAXP, N), I32),
            v((N, width), BF),
            v((N, width), BF),
            v((N, width), BF),
            v((CW, width), BF),
            v((CW, width), BF),
            v((PAGE, 2, PAGE, CW), BF),
            v((N, CW, MAXP * PAGE), BF),
            v((N, CW, PAGE), BF),
            v((ROWS, CW), BF),
            v((ROWS, CW), BF),
            v((ROWS, CW), BF),
            v((ROWS, CW), BF),
            v((N, 128), I32),
            v((N, 128), I32),
            pltpu.SMEM((N, 128), I32),
            v((Z, N, 128), F32),
            v((ROWS, HD), BF),
            v((ROWS, HD), BF),
            v((ROWS, HD), BF),
            v((ROWS, HD), BF),
            v((N, 128), F32),
            v((N, 128), F32),
            v((128, 128), BF),
            v((ROWS, ROWS), BF),
            v((2 * ROWS, ROWS), BF),
            v((ROWS, N), BF),
            v((ROWS, 128), F32),
            v((ROWS, CW), BF),
            v((ROWS, HD), F32),
            v((ROWS, HD), F32),
            v((ROWS, CW), BF),
            v((ROWS, CW), F32),
            v((ROWS, ROWS), F32),
            v((ROWS, ROWS), BF),
            v((ROWS, ROWS), F32),
            v((ROWS, PAGE), F32),
            v((128, 128), F32),
            v((ROWS, HD), F32),
            v((ROWS, 128), F32),
            v((ROWS, CW), BF),
            pltpu.SemaphoreType.DMA((18,)),
            pltpu.SemaphoreType.DMA((7,)),
            pltpu.SemaphoreType.DMA((7,)),
            pltpu.SemaphoreType.DMA((5,)),
        ],
        compiler_params=pltpu.CompilerParams(
            collective_id=0, has_side_effects=True, vmem_limit_bytes=63 * 1024 * 1024
        ),
    )(
        adapter_owner_map.T,
        adapter_fetch_table,
        table,
        page_transfer_table,
        page_entry_mask.T,
        lengths.reshape(1, N),
        fresh_key_value,
        hidden,
        base_query_projection,
        adapter_down_panels.reshape(CW, width),
        adapter_up_panels.reshape(CW, width),
        key_value_page_cache,
    )


def solution(mesh):
    return jax.shard_map(
        shards,
        mesh=mesh,
        in_specs=(
            P("dp", "mp"),
            P("dp", "mp"),
            P("dp", None),
            P("dp", None),
            P("dp", None, "mp"),
            P("dp", None, "mp"),
            P("dp", None, None, "mp"),
            P("dp", None),
            P("dp", None),
            P("dp", None),
            P("dp"),
            P("dp", None, "mp"),
        ),
        out_specs=P("dp", "mp"),
        check_vma=False,
    )
```
